32 devices in a mesh: groups: 2 (over y), row: 4 (over z), col: 2 (over x), sub: 2 (over core).
Axes of the slice: x: 2, y: 2, z: 4, core: 2. Of those that a mesh axis runs over, the one named last changes fastest.
Arguments:
- pixels: bfloat16 [4, 4096, 2048], P('groups', ('row', 'col', 'sub')), parts along dimension 0, may hold values from 0.019897461 to 1
Outputs:
- phase: float32 [4, 512, 256], P(('groups', 'sub'), 'row', 'col'), parts along dimension 0
- mean_flux: float32 [4, 512, 256], P(('groups', 'sub'), 'row', 'col'), parts along dimension 0
- spot_size: float32 [4, 512, 256], P(('groups', 'sub'), 'row', 'col'), parts along dimension 0
The draws below stay inside these ranges and needn't reach their ends.
There are 2 independent parts, one for each index of `groups`. The reference program is written for one: setup_inputs(seed, part) draws one part's arguments, and reference() takes and returns one part's arrays. A program takes and returns all parts, laid end to end along the dimension named above; each array names one. Nothing has to cross between parts.
All inputs are finite; a program needn't handle non-finite values.
Results may differ from the reference program's by a relative error of at most 0.0011.
Values sent between devices are 32-bit elements; how exact they have to be, the bound alone decides.
A program may use at most 128 MiB of HBM per device.

```python
import math
import jax
import jax.numpy as jnp
from jax import lax

PIX = 8
SUBN = 128
MARGIN = 8
FRAMES = 2
NR = 512
NC = 256
N_ROW = 4
N_COL = 2


def steps_of(stream_key, extent, cuts, least, high):
    factor_of = 1.0
    for position, shards_of in cuts:
        heights = jax.random.uniform(jax.random.fold_in(jax.random.fold_in(stream_key, 6), position), (shards_of,), jnp.float32, least / len(cuts), high / len(cuts))
        factor_of = factor_of * jnp.repeat(jnp.exp(heights), extent[position] // shards_of).reshape((-1,) + (1,) * (len(extent) - 1 - position))
    return factor_of


def setup_inputs(seed: int = 0, part: int = 0) -> dict:
    splits = jax.random.split(jax.random.key(seed), 2)
    part_keys = jax.random.split(jax.random.fold_in(splits[1], part), 2)
    pixels = jnp.clip(jnp.exp(math.log(1.0) - 3.9171631 * jax.random.uniform(part_keys[0], (FRAMES, NR * PIX, NC * PIX), jnp.float32) ** steps_of(part_keys[0], (FRAMES, NR * PIX, NC * PIX), ((1, 16),), -0.2, 0.2)), 0.019897461, 1.0).astype(jnp.bfloat16)
    return {"pixels": pixels}


damping = 2e-05

def moment_table():
    offset = jnp.arange(PIX, dtype=jnp.float32) - (PIX - 1) / 2.0
    table = jnp.stack([jnp.ones_like(offset), offset, offset * offset], 1)
    return (table, offset)

def make_basis(count):
    order = jnp.arange(1, count + 1, dtype=jnp.float32)
    angles = math.pi * order[:, None] * order[None, :] / (count + 1)
    vectors = jnp.sqrt(2.0 / (count + 1)) * jnp.sin(angles)
    spectrum = 2.0 - 2.0 * jnp.cos(math.pi * order / (count + 1))
    return (vectors, spectrum[:, None] + spectrum[None, :] + damping)

def coarse_matrix(blocks_down, blocks_across):
    number = blocks_down * blocks_across
    labels = jnp.arange(number, dtype=jnp.int32)
    block_row = labels // blocks_across
    block_col = labels % blocks_across
    apart = jnp.abs(block_row[:, None] - block_row[None, :]) + jnp.abs(block_col[:, None] - block_col[None, :])
    touching = (apart == 1).astype(jnp.float32)
    laplace = jnp.diag(lax.optimization_barrier(jnp.sum(touching, 1))) - touching
    return SUBN * laplace + damping * SUBN * SUBN * jnp.eye(number, dtype=jnp.float32)

def solve_window(window, vectors, denominator):
    highest = lax.Precision.HIGHEST
    inner = jnp.dot(jnp.dot(vectors, window, precision=highest), vectors, precision=highest)
    inner = inner / denominator
    return jnp.dot(jnp.dot(vectors, inner, precision=highest), vectors, precision=highest)

def divergence(flow_x, flow_y):
    from_left = jnp.pad(flow_x, ((0, 0), (1, 0)))[:, :-1]
    from_above = jnp.pad(flow_y, ((1, 0), (0, 0)))[:-1, :]
    return from_left - flow_x + from_above - flow_y

def one_frame(readout):
    table, offset = moment_table()
    blocks = readout.astype(jnp.float32).reshape(NR, PIX, NC, PIX)
    partial_value = jnp.einsum('iajb,bk->kiaj', blocks, table)
    intensity = lax.optimization_barrier(jnp.sum(partial_value[0], 1))
    moment_x = lax.optimization_barrier(jnp.sum(partial_value[1], 1))
    moment_y = lax.optimization_barrier(jnp.sum(partial_value[0] * offset[None, :, None], 1))
    moment_two = lax.optimization_barrier(jnp.sum(partial_value[2], 1)) + lax.optimization_barrier(jnp.sum(partial_value[0] * (offset * offset)[None, :, None], 1))
    slope_x = moment_x / intensity
    slope_y = moment_y / intensity
    spot_size = moment_two / intensity - slope_x * slope_x - slope_y * slope_y
    mean_flux = intensity / (PIX * PIX)
    column = jnp.arange(NC, dtype=jnp.int32)
    rowline = jnp.arange(NR, dtype=jnp.int32)
    flow_x = jnp.where(column[None, :] < NC - 1, slope_x, 0.0)
    flow_y = jnp.where(rowline[:, None] < NR - 1, slope_y, 0.0)
    source = divergence(flow_x, flow_y)
    coarse_rhs = lax.optimization_barrier(jnp.sum(source.reshape(N_ROW, SUBN, N_COL, SUBN), (1, 3))).reshape(-1)
    factor = jnp.linalg.cholesky(coarse_matrix(N_ROW, N_COL))
    coarse_phase = jax.scipy.linalg.cho_solve((factor, True), coarse_rhs)
    count = SUBN + 2 * MARGIN
    vectors, denominator = make_basis(count)
    padded = jnp.pad(source, MARGIN)

    def add_block(label, summed):
        start_row = (label // N_COL * SUBN).astype(jnp.int32)
        start_col = (label % N_COL * SUBN).astype(jnp.int32)
        window = lax.dynamic_slice(padded, (start_row, start_col), (count, count))
        solved = solve_window(window, vectors, denominator)
        current = lax.dynamic_slice(summed, (start_row, start_col), (count, count))
        return lax.dynamic_update_slice(summed, current + solved, (start_row, start_col))
    summed = lax.fori_loop(0, N_ROW * N_COL, add_block, jnp.zeros(padded.shape, jnp.float32))
    coarse_field = jnp.repeat(jnp.repeat(coarse_phase.reshape(N_ROW, N_COL), SUBN, 0), SUBN, 1)
    phase = summed[MARGIN:MARGIN + NR, MARGIN:MARGIN + NC] + coarse_field
    return (phase, mean_flux, spot_size)

def reference(pixels):
    phase, mean_flux, spot_size = lax.map(one_frame, pixels)
    return (phase, mean_flux, spot_size)
```

```python
import functools
import math

import jax
import jax.numpy as jnp
import numpy as np
from jax import lax
from jax.experimental import pallas as pl
from jax.experimental.pallas import tpu as pltpu
from jax.sharding import PartitionSpec as P

PIX = 8
SUBN = 128
MARGIN = 8
SIDE = SUBN + 2 * MARGIN
damping = 2e-05
MESH = pl.DeviceIdType.MESH


def split_bf16(values):
    high = values.astype(jnp.bfloat16)
    return high, (values - high.astype(jnp.float32)).astype(jnp.bfloat16)


def dot(left, right, contract=((1,), (0,))):
    return lax.dot_general(left, right, (contract, ((), ())), preferred_element_type=jnp.float32)


def dot_three(left, right, contract=((1,), (0,))):
    (left_high, left_low), (right_high, right_low) = left, right
    return (
        dot(left_high, right_high, contract)
        + dot(left_low, right_high, contract)
        + dot(left_high, right_low, contract)
    )


def host_split(values):
    high = values.astype(jnp.bfloat16)
    low = (values - high.astype(np.float64)).astype(jnp.bfloat16)
    return np.stack([high, low])


def host_tables():
    order = np.arange(1, SIDE + 1, dtype=np.float64)
    vectors = np.sqrt(2.0 / (SIDE + 1)) * np.sin(math.pi * np.outer(order, order) / (SIDE + 1))
    spectrum = 2.0 - 2.0 * np.cos(math.pi * order / (SIDE + 1))
    inverse = 1.0 / (spectrum[:, None] + spectrum[None, :] + damping)
    corner = np.zeros((SIDE, SUBN))
    corner[:, :MARGIN] = vectors[:, SUBN + MARGIN :]
    corner[:, SUBN - MARGIN :] = vectors[:, :MARGIN]
    last = np.concatenate([vectors[:, MARGIN : MARGIN + SUBN], corner], 1)
    rims = np.concatenate([vectors[:MARGIN], vectors[SUBN + MARGIN :]], 0)
    return (
        host_split(vectors),
        host_split(last),
        host_split(rims),
        inverse.astype(np.float32),
    )


def coarse_inverse(blocks_down, blocks_across):
    number = blocks_down * blocks_across
    labels = np.arange(number)
    down, across = labels // blocks_across, labels % blocks_across
    apart = np.abs(down[:, None] - down[None, :]) + np.abs(across[:, None] - across[None, :])
    touching = (apart == 1).astype(np.float64)
    laplace = np.diag(touching.sum(1)) - touching
    matrix = SUBN * laplace + damping * SUBN * SUBN * np.eye(number)
    root = np.linalg.inv(np.linalg.cholesky(matrix))
    return (root.T @ root).astype(np.float32)


def each(count, step):
    if count <= 16:
        for index in range(1, count):
            step(index)
    else:
        pl.loop(1, count)(step)


def kernel(
    sizes,
    pixels,
    basis,
    last,
    rims,
    inverse,
    coarse,
    phase,
    flux,
    spot,
    loaded,
    pick_one,
    pick_two,
    parts,
    extras,
    stripes,
    above,
    below,
    second,
    sums,
    rim_out,
    row_out,
    side_in,
    row_in,
    load_sem,
    own_sem,
    part_sem,
    extra_sem,
    edge_sem,
    sum_sem,
    fold_sem,
):
    rows, cols, cores = sizes
    frames, pixel_rows, pixel_cols = pixels.shape
    high = pixel_rows // PIX
    wide = pixel_cols // PIX
    team = cols * cores
    blocks = rows * cols
    chunk = SUBN * PIX
    row, col, core = (lax.axis_index(name) for name in ("row", "col", "sub"))
    seat = col * cores + core
    block = row * cols + col

    def load(frame, tile):
        lanes = pl.ds(tile * chunk, chunk)
        return pltpu.make_async_copy(
            pixels.at[frame, :, lanes], loaded.at[frame, :, lanes], load_sem.at[frame, tile]
        )

    for frame in range(frames):
        for tile in range(cols):
            load(frame, tile).start()

    for ref in (above, below, second, side_in, row_in):
        ref[...] = jnp.zeros_like(ref)

    barrier = pltpu.get_barrier_semaphore()
    everyone = rows * team
    here = row * team + seat

    def greet(step):
        other = lax.rem(here + step, everyone)
        pl.semaphore_signal(
            barrier,
            inc=1,
            device_id={
                "row": other // team,
                "col": lax.rem(other, team) // cores,
                "sub": lax.rem(other, cores),
            },
            device_id_type=MESH,
        )

    each(everyone, greet)

    pixel = lax.broadcasted_iota(jnp.int32, (chunk, SUBN), 0)
    lane = lax.broadcasted_iota(jnp.int32, (chunk, SUBN), 1)
    inside = (pixel >> 3) == lane
    offset = (pixel & 7).astype(jnp.float32) - (PIX - 1) / 2.0
    pick_one[...] = jnp.where(inside, 1.0, 0.0).astype(jnp.bfloat16)
    pick_two[:, :SUBN] = jnp.where(inside, offset, 0.0).astype(jnp.bfloat16)
    pick_two[:, SUBN:] = jnp.where(inside, offset * offset, 0.0).astype(jnp.bfloat16)
    line = lax.broadcasted_iota(jnp.int32, (high, pixel_rows), 0)
    pixel = lax.broadcasted_iota(jnp.int32, (high, pixel_rows), 1)
    inside = (pixel >> 3) == line
    offset = (pixel & 7).astype(jnp.float32) - (PIX - 1) / 2.0
    gather = jnp.concatenate(
        [
            jnp.where(inside, 1.0, 0.0),
            jnp.where(inside, offset, 0.0),
            jnp.where(inside, offset * offset, 0.0),
        ],
        0,
    ).astype(jnp.bfloat16)

    line = lax.broadcasted_iota(jnp.int32, (high, wide), 0)
    column = lax.broadcasted_iota(jnp.int32, (high, wide), 1)
    stripe = row * team + seat
    for frame in range(frames):
        x_tiles, y_tiles = [], []
        for tile in range(cols):
            load(frame, tile).wait()
            lanes = slice(tile * SUBN, (tile + 1) * SUBN)
            summed = dot(gather, loaded[frame, :, tile * chunk : (tile + 1) * chunk])
            near, far = split_bf16(summed)
            ones = dot(near, pick_one[...]) + dot(far, pick_one[...])
            twos = dot(near[:high], pick_two[...]) + dot(far[:high], pick_two[...])
            intensity = ones[:high]
            scale = 1.0 / intensity
            slope_x = twos[:, :SUBN] * scale
            slope_y = ones[high : 2 * high] * scale
            moment_two = twos[:, SUBN:] + ones[2 * high :]
            extras[frame, 0, :, lanes] = intensity * (1.0 / (PIX * PIX))
            extras[frame, 1, :, lanes] = moment_two * scale - slope_x * slope_x - slope_y * slope_y
            x_tiles.append(slope_x)
            y_tiles.append(slope_y)
        flow_x = jnp.where(column < wide - 1, jnp.concatenate(x_tiles, 1), 0.0)
        flow_y = jnp.where(
            stripe * high + line < rows * SUBN - 1, jnp.concatenate(y_tiles, 1), 0.0
        )
        over = pltpu.roll(flow_y, 1, 0)
        source = pltpu.roll(flow_x, 1, 1) - flow_x - flow_y + jnp.where(line > 0, over, 0.0)
        carried = jnp.where(line == 0, over, 0.0)[:MARGIN]
        both = jnp.concatenate([source, carried], 0)
        both = jnp.concatenate([both, jnp.zeros((high + MARGIN, SUBN), jnp.float32)], 1)
        parts[frame] = pltpu.roll(both, MARGIN, 1)

    pl.semaphore_wait(barrier, everyone - 1)

    def window(across):
        return pl.ds(pl.multiple_of(across * SUBN, SUBN), 2 * SUBN)

    def square(across):
        return pl.ds(pl.multiple_of(across * SUBN, SUBN), SUBN)

    def part_copy(step):
        to = lax.rem(seat + step, team)
        across, frame = to // cores, lax.rem(to, cores)
        return pltpu.make_async_remote_copy(
            src_ref=parts.at[frame, :, window(across)],
            dst_ref=stripes.at[seat],
            send_sem=part_sem.at[0, step],
            recv_sem=part_sem.at[1, step],
            device_id={"col": across, "sub": frame},
            device_id_type=MESH,
        )

    def extra_copy(kind, step):
        to = lax.rem(seat + step, team)
        across, frame = to // cores, lax.rem(to, cores)
        return pltpu.make_async_remote_copy(
            src_ref=extras.at[frame, kind, :, square(across)],
            dst_ref=(flux, spot)[kind].at[0, pl.ds(pl.multiple_of(seat * high, 8), high), :],
            send_sem=extra_sem.at[kind, 0, step],
            recv_sem=extra_sem.at[kind, 1, step],
            device_id={"col": across, "sub": frame},
            device_id_type=MESH,
        )

    def edge_copy(which, to):
        across, frame = to // cores, lax.rem(to, cores)
        lines = (
            pl.ds(0, MARGIN),
            pl.ds(high - MARGIN, 2 * MARGIN),
            pl.ds(high, MARGIN),
        )[which]
        return pltpu.make_async_remote_copy(
            src_ref=parts.at[frame, lines, window(across)],
            dst_ref=(below, above, second)[which],
            send_sem=edge_sem.at[which, 0, to],
            recv_sem=edge_sem.at[which, 1, 0],
            device_id={"row": row + (-1 if which == 0 else 1), "col": across, "sub": frame},
            device_id_type=MESH,
        )

    edges = [
        (0, (seat == 0) & (row > 0), row < rows - 1),
        (1, (seat == team - 1) & (row < rows - 1), row > 0),
    ]
    if high == MARGIN:
        edges.append((2, (seat == team - 2) & (row < rows - 1), row > 0))

    each(team, lambda step: part_copy(step).start())
    for which, sends, _ in edges:

        @pl.when(sends)
        def _():
            for to in range(team):
                edge_copy(which, to).start()

    each(team, lambda step: extra_copy(0, step).start())
    each(team, lambda step: extra_copy(1, step).start())
    own_lines = pl.ds(pl.multiple_of(seat * high, 8), high)
    own_copies = [
        pltpu.make_async_copy(
            extras.at[core, kind, :, square(col)], ref.at[0, own_lines, :], own_sem.at[kind]
        )
        for kind, ref in enumerate((flux, spot))
    ]
    for copy in own_copies:
        copy.start()
    stripes[seat] = parts[core, :, window(col)]

    each(team, lambda step: part_copy(step).wait_recv())
    for which, _, receives in edges:

        @pl.when(receives)
        def _():
            edge_copy(which, 0).wait_recv()

    top = above[:MARGIN]
    if high == MARGIN:
        top = top + second[...]
    tiles = [top]
    carry = above[MARGIN:]
    for index in range(team):
        tiles.append(stripes[index, :MARGIN] + carry)
        if high > MARGIN:
            tiles.append(stripes[index, MARGIN:high])
        carry = stripes[index, high:]
    tiles.append(below[...] + carry)
    total = jnp.concatenate(tiles, 0)
    middle = jnp.sum(total[MARGIN : MARGIN + SUBN].reshape(SUBN // 8, 8, 2 * SUBN), 0)
    lane = lax.broadcasted_iota(jnp.int32, (8, SUBN), 1)
    sums[block] = jnp.where(lane < MARGIN, middle[:, SUBN:], middle[:, :SUBN])

    def sum_copy(step):
        to = lax.rem(block + step, blocks)
        return pltpu.make_async_remote_copy(
            src_ref=sums.at[block],
            dst_ref=sums.at[block],
            send_sem=sum_sem.at[0, step],
            recv_sem=sum_sem.at[1, step],
            device_id={"row": to // cols, "col": lax.rem(to, cols)},
            device_id_type=MESH,
        )

    each(blocks, lambda step: sum_copy(step).start())

    vectors = (basis[0], basis[1])
    data = split_bf16(total[:, :SIDE])
    data = split_bf16(dot_three(data, vectors))
    data = dot_three(vectors, data) * inverse[...]
    data = split_bf16(dot_three(vectors, split_bf16(data)))
    sides = dot_three(
        (rims[0], rims[1]),
        (data[0][MARGIN : MARGIN + SUBN], data[1][MARGIN : MARGIN + SUBN]),
        ((1,), (1,)),
    )
    rim_out[...] = sides
    solved = dot_three(data, (last[0], last[1]))
    for index, lines in enumerate((slice(0, MARGIN), slice(SUBN + MARGIN, SIDE))):
        ends = solved[lines, SUBN:]
        row_out[index, 0] = jnp.where(lane >= SUBN - MARGIN, ends, 0.0)
        row_out[index, 1] = solved[lines, :SUBN]
        row_out[index, 2] = jnp.where(lane < MARGIN, ends, 0.0)

    moves = []
    for down in (-1, 0, 1):
        for right in (-1, 0, 1):
            if down == 0 and right == 0:
                continue
            number = (down + 1) * 3 + right + 1
            if down == 0:
                src = rim_out.at[pl.ds(MARGIN if right > 0 else 0, MARGIN)]
                dst = side_in.at[pl.ds(0 if right > 0 else SUBN - MARGIN, MARGIN)]
            else:
                src = row_out.at[(down + 1) // 2, right + 1]
                dst = row_in.at[(down + 1) // 2, right + 1]
            copy = pltpu.make_async_remote_copy(
                src_ref=src,
                dst_ref=dst,
                send_sem=fold_sem.at[0, number],
                recv_sem=fold_sem.at[1, number],
                device_id={"row": row + down, "col": col + right},
                device_id_type=MESH,
            )

            def exists(sign):
                test = row >= 0
                if down:
                    at = row + sign * down
                    test = test & (at >= 0) & (at < rows)
                if right:
                    at = col + sign * right
                    test = test & (at >= 0) & (at < cols)
                return test

            moves.append((copy, exists(1), exists(-1)))

    for copy, sends, _ in moves:
        pl.when(sends)(copy.start)

    each(blocks, lambda step: sum_copy(step).wait_recv())
    mix = sums[0] * coarse[block, 0]
    for index in range(1, blocks):
        mix = mix + sums[index] * coarse[block, index]
    lift = jnp.sum(jnp.sum(mix, 0, keepdims=True), 1, keepdims=True)
    mine = solved[MARGIN : MARGIN + SUBN, :SUBN] + lift

    for copy, _, receives in moves:
        pl.when(receives)(copy.wait_recv)
    mine = mine + side_in[...].T
    phase[0] = jnp.concatenate(
        [
            mine[:MARGIN] + row_in[1, 0] + row_in[1, 1] + row_in[1, 2],
            mine[MARGIN : SUBN - MARGIN],
            mine[SUBN - MARGIN :] + row_in[0, 0] + row_in[0, 1] + row_in[0, 2],
        ],
        0,
    )

    for copy in own_copies:
        copy.wait()
    for kind in range(2):
        each(team, lambda step: extra_copy(kind, step).wait())
    each(team, lambda step: part_copy(step).wait_send())
    for which, sends, _ in edges:

        @pl.when(sends)
        def _():
            for to in range(team):
                edge_copy(which, to).wait_send()

    each(blocks, lambda step: sum_copy(step).wait_send())
    for copy, sends, _ in moves:
        pl.when(sends)(copy.wait_send)


def body(sizes, pixels):
    rows, cols, cores = sizes
    frames, pixel_rows, pixel_cols = pixels.shape
    high = pixel_rows // PIX
    wide = pixel_cols // PIX
    team = cols * cores
    blocks = rows * cols
    vmem = pl.BlockSpec(memory_space=pltpu.VMEM)
    hbm = pl.BlockSpec(memory_space=pl.ANY)
    square = jax.ShapeDtypeStruct((1, SUBN, SUBN), jnp.float32)
    basis, last, rims, inverse = host_tables()
    dma = pltpu.SemaphoreType.DMA
    return pl.pallas_call(
        functools.partial(kernel, sizes),
        out_shape=(square, square, square),
        in_specs=[hbm, vmem, vmem, vmem, vmem, pl.BlockSpec(memory_space=pltpu.SMEM)],
        out_specs=(vmem, hbm, hbm),
        scratch_shapes=[
            pltpu.VMEM((frames, pixel_rows, pixel_cols), jnp.bfloat16),
            pltpu.VMEM((SUBN * PIX, SUBN), jnp.bfloat16),
            pltpu.VMEM((SUBN * PIX, 2 * SUBN), jnp.bfloat16),
            pltpu.VMEM((frames, high + MARGIN, wide + SUBN), jnp.float32),
            pltpu.VMEM((frames, 2, high, wide), jnp.float32),
            pltpu.VMEM((team, high + MARGIN, 2 * SUBN), jnp.float32),
            pltpu.VMEM((2 * MARGIN, 2 * SUBN), jnp.float32),
            pltpu.VMEM((MARGIN, 2 * SUBN), jnp.float32),
            pltpu.VMEM((MARGIN, 2 * SUBN), jnp.float32),
            pltpu.VMEM((blocks, 8, SUBN), jnp.float32),
            pltpu.VMEM((2 * MARGIN, SUBN), jnp.float32),
            pltpu.VMEM((2, 3, MARGIN, SUBN), jnp.float32),
            pltpu.VMEM((SUBN, SUBN), jnp.float32),
            pltpu.VMEM((2, 3, MARGIN, SUBN), jnp.float32),
            dma((frames, cols)),
            dma((2,)),
            dma((2, team)),
            dma((2, 2, team)),
            dma((3, 2, team)),
            dma((2, blocks)),
            dma((2, 9)),
        ],
        compiler_params=pltpu.CompilerParams(
            collective_id=0, has_side_effects=True, vmem_limit_bytes=48 * 1024 * 1024
        ),
        name="schwarz",
    )(pixels, basis, last, rims, inverse, coarse_inverse(rows, cols))


def solution(mesh):
    sizes = tuple(mesh.shape[name] for name in ("row", "col", "sub"))
    out = P(("groups", "sub"), "row", "col")
    return jax.shard_map(
        functools.partial(body, sizes),
        mesh=mesh,
        in_specs=(P("groups", ("row", "col", "sub"), None),),
        out_specs=(out, out, out),
        check_vma=False,
    )
```

```python
import functools
import math

import jax
import jax.numpy as jnp
import numpy as np
from jax import lax
from jax.experimental import pallas as pl
from jax.experimental.pallas import tpu as pltpu
from jax.sharding import PartitionSpec as P

PIX = 8
SUBN = 128
MARGIN = 8
SIDE = SUBN + 2 * MARGIN
damping = 2e-05
MESH = pl.DeviceIdType.MESH


def split_bf16(values):
    high = values.astype(jnp.bfloat16)
    return high, (values - high.astype(jnp.float32)).astype(jnp.bfloat16)


def dot(left, right, contract=((1,), (0,))):
    return lax.dot_general(left, right, (contract, ((), ())), preferred_element_type=jnp.float32)


def dot_three(left, right, contract=((1,), (0,))):
    (left_high, left_low), (right_high, right_low) = left, right
    return (
        dot(left_high, right_high, contract)
        + dot(left_low, right_high, contract)
        + dot(left_high, right_low, contract)
    )


def host_tables():
    order = np.arange(1, SIDE + 1, dtype=np.float64)
    vectors = np.sqrt(2.0 / (SIDE + 1)) * np.sin(math.pi * np.outer(order, order) / (SIDE + 1))
    spectrum = 2.0 - 2.0 * np.cos(math.pi * order / (SIDE + 1))
    inverse = 1.0 / (spectrum[:, None] + spectrum[None, :] + damping)
    corner = np.zeros((SIDE, SUBN))
    corner[:, :MARGIN] = vectors[:, SUBN + MARGIN :]
    corner[:, SUBN - MARGIN :] = vectors[:, :MARGIN]
    last = np.concatenate([vectors[:, MARGIN : MARGIN + SUBN], corner], 1)
    rims = np.concatenate([vectors[:MARGIN], vectors[SUBN + MARGIN :]], 0)
    wide = [np.pad(part, ((0, 0), (0, 2 * SUBN - part.shape[1]))) for part in (vectors, inverse, rims)]
    return np.concatenate([wide[0], last, wide[1], wide[2]], 0).astype(np.float32)


def coarse_inverse(blocks_down, blocks_across):
    number = blocks_down * blocks_across
    labels = np.arange(number)
    down, across = labels // blocks_across, labels % blocks_across
    apart = np.abs(down[:, None] - down[None, :]) + np.abs(across[:, None] - across[None, :])
    touching = (apart == 1).astype(np.float64)
    laplace = np.diag(touching.sum(1)) - touching
    matrix = SUBN * laplace + damping * SUBN * SUBN * np.eye(number)
    root = np.linalg.inv(np.linalg.cholesky(matrix))
    spare = max(SUBN - number, 0)
    return np.pad(root.T @ root, ((0, 0), (0, spare))).astype(np.float32)


def each(count, step):
    if count <= 16:
        for index in range(1, count):
            step(index)
    else:
        pl.loop(1, count)(step)


def kernel(
    sizes,
    pixels,
    constants,
    phase,
    flux,
    spot,
    loaded,
    tables,
    coarse,
    pick_one,
    pick_two,
    parts,
    extras,
    stripes,
    above,
    below,
    second,
    sums,
    rim_out,
    row_out,
    side_in,
    row_in,
    load_sem,
    table_sem,
    part_sem,
    extra_sem,
    edge_sem,
    sum_sem,
    fold_sem,
):
    rows, cols, cores = sizes
    frames, pixel_rows, pixel_cols = pixels.shape
    high = pixel_rows // PIX
    wide = pixel_cols // PIX
    team = cols * cores
    blocks = rows * cols
    chunk = SUBN * PIX
    row, col, core = (lax.axis_index(name) for name in ("row", "col", "sub"))
    seat = col * cores + core
    block = row * cols + col

    def load(frame, tile):
        lanes = pl.ds(tile * chunk, chunk)
        return pltpu.make_async_copy(
            pixels.at[frame, :, lanes], loaded.at[frame, :, lanes], load_sem.at[frame, tile]
        )

    for frame in range(frames):
        for tile in range(cols):
            load(frame, tile).start()
    fetches = [
        pltpu.make_async_copy(far, near, table_sem.at[index])
        for index, (far, near) in enumerate(
            (
                (constants.at[pl.ds(0, tables.shape[0])], tables),
                (
                    constants.at[
                        pl.ds(tables.shape[0], coarse.shape[0]), pl.ds(0, coarse.shape[1])
                    ],
                    coarse,
                ),
            )
        )
    ]
    for copy in fetches:
        copy.start()

    for ref in (above, below, second, side_in, row_in):
        ref[...] = jnp.zeros_like(ref)

    barrier = pltpu.get_barrier_semaphore()
    everyone = rows * team
    here = row * team + seat

    def greet(step):
        other = lax.rem(here + step, everyone)
        pl.semaphore_signal(
            barrier,
            inc=1,
            device_id={
                "row": other // team,
                "col": lax.rem(other, team) // cores,
                "sub": lax.rem(other, cores),
            },
            device_id_type=MESH,
        )

    each(everyone, greet)

    pixel = lax.broadcasted_iota(jnp.int32, (chunk, SUBN), 0)
    lane = lax.broadcasted_iota(jnp.int32, (chunk, SUBN), 1)
    inside = (pixel >> 3) == lane
    offset = (pixel & 7).astype(jnp.float32) - (PIX - 1) / 2.0
    pick_one[...] = jnp.where(inside, 1.0, 0.0).astype(jnp.bfloat16)
    pick_two[:, :SUBN] = jnp.where(inside, offset, 0.0).astype(jnp.bfloat16)
    pick_two[:, SUBN:] = jnp.where(inside, offset * offset, 0.0).astype(jnp.bfloat16)
    line = lax.broadcasted_iota(jnp.int32, (high, pixel_rows), 0)
    pixel = lax.broadcasted_iota(jnp.int32, (high, pixel_rows), 1)
    inside = (pixel >> 3) == line
    offset = (pixel & 7).astype(jnp.float32) - (PIX - 1) / 2.0
    gather = jnp.concatenate(
        [
            jnp.where(inside, 1.0, 0.0),
            jnp.where(inside, offset, 0.0),
            jnp.where(inside, offset * offset, 0.0),
        ],
        0,
    ).astype(jnp.bfloat16)

    def window(across):
        return pl.ds(pl.multiple_of(across * SUBN, SUBN), 2 * SUBN)

    def square(across):
        return pl.ds(pl.multiple_of(across * SUBN, SUBN), SUBN)

    def part_copy(frame, across):
        return pltpu.make_async_remote_copy(
            src_ref=parts.at[frame, :, window(across)],
            dst_ref=stripes.at[seat],
            send_sem=part_sem.at[0, frame, across],
            recv_sem=part_sem.at[1, core, col],
            device_id={"col": across, "sub": frame},
            device_id_type=MESH,
        )

    own_lines = pl.ds(pl.multiple_of(seat * high, 8), high)

    def extra_copy(kind, frame, across):
        return pltpu.make_async_remote_copy(
            src_ref=extras.at[frame, kind, :, square(across)],
            dst_ref=(flux, spot)[kind].at[0, own_lines, :],
            send_sem=extra_sem.at[kind, 0, frame, across],
            recv_sem=extra_sem.at[kind, 1, core, col],
            device_id={"col": across, "sub": frame},
            device_id_type=MESH,
        )

    def edge_copy(which, frame, across):
        lines = (
            pl.ds(0, MARGIN),
            pl.ds(high - MARGIN, 2 * MARGIN),
            pl.ds(high, MARGIN),
        )[which]
        return pltpu.make_async_remote_copy(
            src_ref=parts.at[frame, lines, window(across)],
            dst_ref=(below, above, second)[which],
            send_sem=edge_sem.at[which, 0, frame, across],
            recv_sem=edge_sem.at[which, 1, 0, 0],
            device_id={"row": row + (-1 if which == 0 else 1), "col": across, "sub": frame},
            device_id_type=MESH,
        )

    edges = [
        (0, (seat == 0) & (row > 0), row < rows - 1),
        (1, (seat == team - 1) & (row < rows - 1), row > 0),
    ]
    if high == MARGIN:
        edges.append((2, (seat == team - 2) & (row < rows - 1), row > 0))

    def members(frame, action):
        for step in range(1, cols):
            action(lax.rem(col + step, cols))
        pl.when(core != frame)(lambda: action(col))

    def senders(action):
        def one(step):
            other = lax.rem(seat + step, team)
            action(lax.rem(other, cores), other // cores)

        each(team, one)

    line = lax.broadcasted_iota(jnp.int32, (high, wide), 0)
    column = lax.broadcasted_iota(jnp.int32, (high, wide), 1)
    stripe = row * team + seat
    for frame in range(frames):
        summed = []
        for tile in range(cols):
            load(frame, tile).wait()
            summed.append(dot(gather, loaded[frame, :, tile * chunk : (tile + 1) * chunk]))
        near, far = split_bf16(
            jnp.concatenate(
                [part[kind * high : (kind + 1) * high] for kind in range(3) for part in summed], 0
            )
        )
        tall = cols * high
        ones = dot(near, pick_one[...]) + dot(far, pick_one[...])
        twos = dot(near[:tall], pick_two[...]) + dot(far[:tall], pick_two[...])
        intensity = ones[:tall]
        scale = 1.0 / intensity
        slope_x = twos[:, :SUBN] * scale
        slope_y = ones[tall : 2 * tall] * scale
        moment_two = twos[:, SUBN:] + ones[2 * tall :]

        def grid(values):
            return jnp.concatenate(
                [values[tile * high : (tile + 1) * high] for tile in range(cols)], 1
            )

        flow_x = jnp.where(column < wide - 1, grid(slope_x), 0.0)
        flow_y = jnp.where(stripe * high + line < rows * SUBN - 1, grid(slope_y), 0.0)
        over = pltpu.roll(flow_y, 1, 0)
        source = pltpu.roll(flow_x, 1, 1) - flow_x - flow_y + jnp.where(line > 0, over, 0.0)
        carried = jnp.where(line == 0, over, 0.0)[:MARGIN]
        both = jnp.concatenate([source, carried], 0)
        both = jnp.concatenate([both, jnp.zeros((high + MARGIN, SUBN), jnp.float32)], 1)
        parts[frame] = pltpu.roll(both, MARGIN, 1)
        if frame == 0:
            pl.semaphore_wait(barrier, everyone - 1)
        members(frame, lambda across: part_copy(frame, across).start())
        for which, sends, _ in edges:

            @pl.when(sends)
            def _():
                for across in range(cols):
                    edge_copy(which, frame, across).start()

        extras[frame, 0] = grid(intensity) * (1.0 / (PIX * PIX))
        extras[frame, 1] = grid(moment_two * scale - slope_x * slope_x - slope_y * slope_y)
        for kind in range(2):
            members(frame, lambda across: extra_copy(kind, frame, across).start())

    stripes[seat] = parts[core, :, window(col)]
    flux[0, own_lines, :] = extras[core, 0, :, square(col)]
    spot[0, own_lines, :] = extras[core, 1, :, square(col)]

    def part_arrival(of_core, of_col):
        return pltpu.make_async_remote_copy(
            src_ref=stripes.at[0],
            dst_ref=stripes.at[0],
            send_sem=part_sem.at[0, 0, 0],
            recv_sem=part_sem.at[1, of_core, of_col],
            device_id={"col": of_col, "sub": of_core},
            device_id_type=MESH,
        )

    def extra_arrival(kind, of_core, of_col):
        lines = pl.ds(0, high)
        return pltpu.make_async_remote_copy(
            src_ref=flux.at[0, lines, :],
            dst_ref=(flux, spot)[kind].at[0, lines, :],
            send_sem=extra_sem.at[kind, 0, 0, 0],
            recv_sem=extra_sem.at[kind, 1, of_core, of_col],
            device_id={"col": of_col, "sub": of_core},
            device_id_type=MESH,
        )

    senders(lambda of_core, of_col: part_arrival(of_core, of_col).wait_recv())
    for which, _, receives in edges:

        @pl.when(receives)
        def _():
            edge_copy(which, 0, 0).wait_recv()

    top = above[:MARGIN]
    if high == MARGIN:
        top = top + second[...]
    tiles = [top]
    carry = above[MARGIN:]
    for index in range(team):
        tiles.append(stripes[index, :MARGIN] + carry)
        if high > MARGIN:
            tiles.append(stripes[index, MARGIN:high])
        carry = stripes[index, high:]
    tiles.append(below[...] + carry)
    total = jnp.concatenate(tiles, 0)
    middle = jnp.sum(total[MARGIN : MARGIN + SUBN].reshape(SUBN // 8, 8, 2 * SUBN), 0)
    lane = lax.broadcasted_iota(jnp.int32, (8, SUBN), 1)
    sums[block] = jnp.where(lane < MARGIN, middle[:, SUBN:], middle[:, :SUBN])

    def sum_copy(step):
        to = lax.rem(block + step, blocks)
        return pltpu.make_async_remote_copy(
            src_ref=sums.at[block],
            dst_ref=sums.at[block],
            send_sem=sum_sem.at[0, step],
            recv_sem=sum_sem.at[1, step],
            device_id={"row": to // cols, "col": lax.rem(to, cols)},
            device_id_type=MESH,
        )

    each(blocks, lambda step: sum_copy(step).start())

    for copy in fetches:
        copy.wait()
    vectors = split_bf16(tables[:SIDE, :SIDE])
    last = split_bf16(tables[SIDE : 2 * SIDE])
    inverse = tables[2 * SIDE : 3 * SIDE, :SIDE]
    rims = split_bf16(tables[3 * SIDE :, :SIDE])
    data = split_bf16(total[:, :SIDE])
    data = split_bf16(dot_three(data, vectors))
    data = dot_three(vectors, data) * inverse
    data = split_bf16(dot_three(vectors, split_bf16(data)))
    sides = dot_three(
        rims,
        (data[0][MARGIN : MARGIN + SUBN], data[1][MARGIN : MARGIN + SUBN]),
        ((1,), (1,)),
    )
    rim_out[...] = sides
    solved = dot_three(data, last)
    for index, lines in enumerate((slice(0, MARGIN), slice(SUBN + MARGIN, SIDE))):
        ends = solved[lines, SUBN:]
        row_out[index, 0] = jnp.where(lane >= SUBN - MARGIN, ends, 0.0)
        row_out[index, 1] = solved[lines, :SUBN]
        row_out[index, 2] = jnp.where(lane < MARGIN, ends, 0.0)

    moves = []
    for down in (-1, 0, 1):
        for right in (-1, 0, 1):
            if down == 0 and right == 0:
                continue
            number = (down + 1) * 3 + right + 1
            if down == 0:
                src = rim_out.at[pl.ds(MARGIN if right > 0 else 0, MARGIN)]
                dst = side_in.at[pl.ds(0 if right > 0 else SUBN - MARGIN, MARGIN)]
            else:
                src = row_out.at[(down + 1) // 2, right + 1]
                dst = row_in.at[(down + 1) // 2, right + 1]
            copy = pltpu.make_async_remote_copy(
                src_ref=src,
                dst_ref=dst,
                send_sem=fold_sem.at[0, number],
                recv_sem=fold_sem.at[1, number],
                device_id={"row": row + down, "col": col + right},
                device_id_type=MESH,
            )

            def exists(sign):
                test = row >= 0
                if down:
                    at = row + sign * down
                    test = test & (at >= 0) & (at < rows)
                if right:
                    at = col + sign * right
                    test = test & (at >= 0) & (at < cols)
                return test

            moves.append((copy, exists(1), exists(-1)))

    for copy, sends, _ in moves:
        pl.when(sends)(copy.start)

    each(blocks, lambda step: sum_copy(step).wait_recv())
    mix = sums[0] * coarse[block, 0]
    for index in range(1, blocks):
        mix = mix + sums[index] * coarse[block, index]
    lift = jnp.sum(jnp.sum(mix, 0, keepdims=True), 1, keepdims=True)
    mine = solved[MARGIN : MARGIN + SUBN, :SUBN] + lift

    for copy, _, receives in moves:
        pl.when(receives)(copy.wait_recv)
    mine = mine + side_in[...].T
    phase[0] = jnp.concatenate(
        [
            mine[:MARGIN] + row_in[1, 0] + row_in[1, 1] + row_in[1, 2],
            mine[MARGIN : SUBN - MARGIN],
            mine[SUBN - MARGIN :] + row_in[0, 0] + row_in[0, 1] + row_in[0, 2],
        ],
        0,
    )

    for kind in range(2):
        senders(lambda of_core, of_col: extra_arrival(kind, of_core, of_col).wait_recv())
    for frame in range(frames):
        members(frame, lambda across: part_copy(frame, across).wait_send())
        for kind in range(2):
            members(frame, lambda across: extra_copy(kind, frame, across).wait_send())
        for which, sends, _ in edges:

            @pl.when(sends)
            def _():
                for across in range(cols):
                    edge_copy(which, frame, across).wait_send()

    each(blocks, lambda step: sum_copy(step).wait_send())
    for copy, sends, _ in moves:
        pl.when(sends)(copy.wait_send)


def deliver(phase, flux, spot, phase_out, flux_out, spot_out, sem):
    copies = [
        pltpu.make_async_copy(near, far, sem.at[index])
        for index, (near, far) in enumerate(
            ((phase, phase_out), (flux, flux_out), (spot, spot_out))
        )
    ]
    for copy in copies:
        copy.start()
    for copy in copies:
        copy.wait()


def body(sizes, pixels):
    rows, cols, cores = sizes
    frames, pixel_rows, pixel_cols = pixels.shape
    high = pixel_rows // PIX
    wide = pixel_cols // PIX
    team = cols * cores
    blocks = rows * cols
    vmem = pl.BlockSpec(memory_space=pltpu.VMEM)
    hbm = pl.BlockSpec(memory_space=pltpu.HBM)
    square = jax.ShapeDtypeStruct((1, SUBN, SUBN), jnp.float32)
    tables = host_tables()
    coarse = coarse_inverse(rows, cols)
    constants = np.zeros((2304, 2 * SUBN), np.float32)
    constants[: tables.shape[0]] = tables
    constants[tables.shape[0] : tables.shape[0] + blocks, : coarse.shape[1]] = coarse
    dma = pltpu.SemaphoreType.DMA
    results = pl.pallas_call(
        functools.partial(kernel, sizes),
        out_shape=(square, square, square),
        in_specs=[hbm] * 2,
        out_specs=(vmem, vmem, vmem),
        scratch_shapes=[
            pltpu.VMEM((frames, pixel_rows, pixel_cols), jnp.bfloat16),
            pltpu.VMEM(tables.shape, jnp.float32),
            pltpu.SMEM(coarse.shape, jnp.float32),
            pltpu.VMEM((SUBN * PIX, SUBN), jnp.bfloat16),
            pltpu.VMEM((SUBN * PIX, 2 * SUBN), jnp.bfloat16),
            pltpu.VMEM((frames, high + MARGIN, wide + SUBN), jnp.float32),
            pltpu.VMEM((frames, 2, high, wide), jnp.float32),
            pltpu.VMEM((team, high + MARGIN, 2 * SUBN), jnp.float32),
            pltpu.VMEM((2 * MARGIN, 2 * SUBN), jnp.float32),
            pltpu.VMEM((MARGIN, 2 * SUBN), jnp.float32),
            pltpu.VMEM((MARGIN, 2 * SUBN), jnp.float32),
            pltpu.VMEM((blocks, 8, SUBN), jnp.float32),
            pltpu.VMEM((2 * MARGIN, SUBN), jnp.float32),
            pltpu.VMEM((2, 3, MARGIN, SUBN), jnp.float32),
            pltpu.VMEM((SUBN, SUBN), jnp.float32),
            pltpu.VMEM((2, 3, MARGIN, SUBN), jnp.float32),
            dma((frames, cols)),
            dma((2,)),
            dma((2, cores, cols)),
            dma((2, 2, cores, cols)),
            dma((3, 2, cores, cols)),
            dma((2, blocks)),
            dma((2, 9)),
        ],
        compiler_params=pltpu.CompilerParams(
            collective_id=0, has_side_effects=True, vmem_limit_bytes=53 * 1024 * 1024
        ),
        name="schwarz",
    )(pixels, constants)
    return pl.pallas_call(
        deliver,
        out_shape=(square, square, square),
        in_specs=[vmem] * 3,
        out_specs=(hbm, hbm, hbm),
        scratch_shapes=[dma((3,))],
        name="deliver",
    )(*results)


def solution(mesh):
    sizes = tuple(mesh.shape[name] for name in ("row", "col", "sub"))
    out = P(("groups", "sub"), "row", "col")
    return jax.shard_map(
        functools.partial(body, sizes),
        mesh=mesh,
        in_specs=(P("groups", ("row", "col", "sub"), None),),
        out_specs=(out, out, out),
        check_vma=False,
    )
```

```python
import functools
import math

import jax
import jax.numpy as jnp
import numpy as np
from jax import lax
from jax.experimental import pallas as pl
from jax.experimental.pallas import tpu as pltpu
from jax.sharding import PartitionSpec as P

PIX = 8
SUBN = 128
MARGIN = 8
SIDE = SUBN + 2 * MARGIN
damping = 2e-05
MESH = pl.DeviceIdType.MESH


def split_bf16(values):
    high = values.astype(jnp.bfloat16)
    return high, (values - high.astype(jnp.float32)).astype(jnp.bfloat16)


def dot(left, right, contract=((1,), (0,))):
    return lax.dot_general(left, right, (contract, ((), ())), preferred_element_type=jnp.float32)


def dot_three(left, right, contract=((1,), (0,))):
    (left_high, left_low), (right_high, right_low) = left, right
    return (
        dot(left_high, right_high, contract)
        + dot(left_low, right_high, contract)
        + dot(left_high, right_low, contract)
    )


def host_tables():
    order = np.arange(1, SIDE + 1, dtype=np.float64)
    vectors = np.sqrt(2.0 / (SIDE + 1)) * np.sin(math.pi * np.outer(order, order) / (SIDE + 1))
    spectrum = 2.0 - 2.0 * np.cos(math.pi * order / (SIDE + 1))
    inverse = 1.0 / (spectrum[:, None] + spectrum[None, :] + damping)
    corner = np.zeros((SIDE, SUBN))
    corner[:, :MARGIN] = vectors[:, SUBN + MARGIN :]
    corner[:, SUBN - MARGIN :] = vectors[:, :MARGIN]
    last = np.concatenate([vectors[:, MARGIN : MARGIN + SUBN], corner], 1)
    rims = np.concatenate([vectors[:MARGIN], vectors[SUBN + MARGIN :]], 0)
    wide = [np.pad(part, ((0, 0), (0, 2 * SUBN - part.shape[1]))) for part in (vectors, inverse, rims)]
    return np.concatenate([wide[0], last, wide[1], wide[2]], 0).astype(np.float32)


def coarse_inverse(blocks_down, blocks_across):
    number = blocks_down * blocks_across
    labels = np.arange(number)
    down, across = labels // blocks_across, labels % blocks_across
    apart = np.abs(down[:, None] - down[None, :]) + np.abs(across[:, None] - across[None, :])
    touching = (apart == 1).astype(np.float64)
    laplace = np.diag(touching.sum(1)) - touching
    matrix = SUBN * laplace + damping * SUBN * SUBN * np.eye(number)
    root = np.linalg.inv(np.linalg.cholesky(matrix))
    spare = max(SUBN - number, 0)
    return np.pad(root.T @ root, ((0, 0), (0, spare))).astype(np.float32)


def each(count, step):
    if count <= 16:
        for index in range(1, count):
            step(index)
    else:
        pl.loop(1, count)(step)


def kernel(
    sizes,
    pixels,
    constants,
    phase,
    flux,
    spot,
    loaded,
    tables,
    halves,
    coarse,
    pick_one,
    pick_two,
    parts,
    extras,
    stripes,
    above,
    below,
    second,
    sums,
    rim_out,
    row_out,
    side_in,
    row_in,
    load_sem,
    table_sem,
    part_sem,
    extra_sem,
    edge_sem,
    sum_sem,
    fold_sem,
):
    rows, cols, cores = sizes
    frames, pixel_rows, pixel_cols = pixels.shape
    high = pixel_rows // PIX
    wide = pixel_cols // PIX
    team = cols * cores
    blocks = rows * cols
    chunk = SUBN * PIX
    row, col, core = (lax.axis_index(name) for name in ("row", "col", "sub"))
    seat = col * cores + core
    block = row * cols + col

    def load(frame, tile):
        lanes = pl.ds(tile * chunk, chunk)
        return pltpu.make_async_copy(
            pixels.at[frame, :, lanes], loaded.at[frame, :, lanes], load_sem.at[frame, tile]
        )

    for frame in range(frames):
        for tile in range(cols):
            load(frame, tile).start()
    fetches = [
        pltpu.make_async_copy(far, near, table_sem.at[index])
        for index, (far, near) in enumerate(
            (
                (constants.at[pl.ds(0, tables.shape[0])], tables),
                (
                    constants.at[
                        pl.ds(tables.shape[0], coarse.shape[0]), pl.ds(0, coarse.shape[1])
                    ],
                    coarse,
                ),
            )
        )
    ]
    for copy in fetches:
        copy.start()

    for ref in (above, below, second, side_in, row_in):
        ref[...] = jnp.zeros_like(ref)

    barrier = pltpu.get_barrier_semaphore()
    everyone = rows * team
    here = row * team + seat

    def greet(step):
        other = lax.rem(here + step, everyone)
        pl.semaphore_signal(
            barrier,
            inc=1,
            device_id={
                "row": other // team,
                "col": lax.rem(other, team) // cores,
                "sub": lax.rem(other, cores),
            },
            device_id_type=MESH,
        )

    each(everyone, greet)

    pixel = lax.broadcasted_iota(jnp.int32, (chunk, SUBN), 0)
    lane = lax.broadcasted_iota(jnp.int32, (chunk, SUBN), 1)
    inside = (pixel >> 3) == lane
    offset = (pixel & 7).astype(jnp.float32) - (PIX - 1) / 2.0
    pick_one[...] = jnp.where(inside, 1.0, 0.0).astype(jnp.bfloat16)
    pick_two[:, :SUBN] = jnp.where(inside, offset, 0.0).astype(jnp.bfloat16)
    pick_two[:, SUBN:] = jnp.where(inside, offset * offset, 0.0).astype(jnp.bfloat16)
    line = lax.broadcasted_iota(jnp.int32, (high, pixel_rows), 0)
    pixel = lax.broadcasted_iota(jnp.int32, (high, pixel_rows), 1)
    inside = (pixel >> 3) == line
    offset = (pixel & 7).astype(jnp.float32) - (PIX - 1) / 2.0
    gather = jnp.concatenate(
        [
            jnp.where(inside, 1.0, 0.0),
            jnp.where(inside, offset, 0.0),
            jnp.where(inside, offset * offset, 0.0),
        ],
        0,
    ).astype(jnp.bfloat16)

    def window(across):
        return pl.ds(pl.multiple_of(across * SUBN, SUBN), 2 * SUBN)

    def square(across):
        return pl.ds(pl.multiple_of(across * SUBN, SUBN), SUBN)

    def part_copy(frame, across):
        return pltpu.make_async_remote_copy(
            src_ref=parts.at[frame, :, window(across)],
            dst_ref=stripes.at[seat],
            send_sem=part_sem.at[0, frame, across],
            recv_sem=part_sem.at[1, core, col],
            device_id={"col": across, "sub": frame},
            device_id_type=MESH,
        )

    own_lines = pl.ds(pl.multiple_of(seat * high, 8), high)

    def extra_copy(kind, frame, across):
        return pltpu.make_async_remote_copy(
            src_ref=extras.at[frame, kind, :, square(across)],
            dst_ref=(flux, spot)[kind].at[0, own_lines, :],
            send_sem=extra_sem.at[kind, 0, frame, across],
            recv_sem=extra_sem.at[kind, 1, core, col],
            device_id={"col": across, "sub": frame},
            device_id_type=MESH,
        )

    def edge_copy(which, frame, across):
        lines = (
            pl.ds(0, MARGIN),
            pl.ds(high - MARGIN, 2 * MARGIN),
            pl.ds(high, MARGIN),
        )[which]
        return pltpu.make_async_remote_copy(
            src_ref=parts.at[frame, lines, window(across)],
            dst_ref=(below, above, second)[which],
            send_sem=edge_sem.at[which, 0, frame, across],
            recv_sem=edge_sem.at[which, 1, 0, 0],
            device_id={"row": row + (-1 if which == 0 else 1), "col": across, "sub": frame},
            device_id_type=MESH,
        )

    edges = [
        (0, (seat == 0) & (row > 0), row < rows - 1),
        (1, (seat == team - 1) & (row < rows - 1), row > 0),
    ]
    if high == MARGIN:
        edges.append((2, (seat == team - 2) & (row < rows - 1), row > 0))

    def members(frame, action):
        for step in range(1, cols):
            action(lax.rem(col + step, cols))
        pl.when(core != frame)(lambda: action(col))

    def senders(action):
        def one(step):
            other = lax.rem(seat + step, team)
            action(lax.rem(other, cores), other // cores)

        each(team, one)

    line = lax.broadcasted_iota(jnp.int32, (high, wide), 0)
    column = lax.broadcasted_iota(jnp.int32, (high, wide), 1)
    stripe = row * team + seat
    for frame in range(frames):
        summed = []
        for tile in range(cols):
            load(frame, tile).wait()
            summed.append(dot(gather, loaded[frame, :, tile * chunk : (tile + 1) * chunk]))
        near, far = split_bf16(
            jnp.concatenate(
                [part[kind * high : (kind + 1) * high] for kind in range(3) for part in summed], 0
            )
        )
        tall = cols * high
        ones = dot(near, pick_one[...]) + dot(far, pick_one[...])
        twos = dot(near[:tall], pick_two[...]) + dot(far[:tall], pick_two[...])
        intensity = ones[:tall]
        scale = 1.0 / intensity
        slope_x = twos[:, :SUBN] * scale
        slope_y = ones[tall : 2 * tall] * scale
        moment_two = twos[:, SUBN:] + ones[2 * tall :]

        def grid(values):
            return jnp.concatenate(
                [values[tile * high : (tile + 1) * high] for tile in range(cols)], 1
            )

        flow_x = jnp.where(column < wide - 1, grid(slope_x), 0.0)
        flow_y = jnp.where(stripe * high + line < rows * SUBN - 1, grid(slope_y), 0.0)
        over = pltpu.roll(flow_y, 1, 0)
        source = pltpu.roll(flow_x, 1, 1) - flow_x - flow_y + jnp.where(line > 0, over, 0.0)
        carried = jnp.where(line == 0, over, 0.0)[:MARGIN]
        both = jnp.concatenate([source, carried], 0)
        both = jnp.concatenate([both, jnp.zeros((high + MARGIN, SUBN), jnp.float32)], 1)
        parts[frame] = pltpu.roll(both, MARGIN, 1)
        if frame == 0:
            pl.semaphore_wait(barrier, everyone - 1)
        members(frame, lambda across: part_copy(frame, across).start())
        for which, sends, _ in edges:

            @pl.when(sends)
            def _():
                for across in range(cols):
                    edge_copy(which, frame, across).start()

        extras[frame, 0] = grid(intensity) * (1.0 / (PIX * PIX))
        extras[frame, 1] = grid(moment_two * scale - slope_x * slope_x - slope_y * slope_y)

    for frame in range(frames):
        for kind in range(2):
            members(frame, lambda across: extra_copy(kind, frame, across).start())

    for copy in fetches:
        copy.wait()
    for lines, source_lines in (
        (slice(0, 2 * SIDE), slice(0, 2 * SIDE)),
        (slice(2 * SIDE, 2 * SIDE + 2 * MARGIN), slice(3 * SIDE, 3 * SIDE + 2 * MARGIN)),
    ):
        halves[0, lines], halves[1, lines] = split_bf16(tables[source_lines])

    stripes[seat] = parts[core, :, window(col)]
    flux[0, own_lines, :] = extras[core, 0, :, square(col)]
    spot[0, own_lines, :] = extras[core, 1, :, square(col)]

    def part_arrival(of_core, of_col):
        return pltpu.make_async_remote_copy(
            src_ref=stripes.at[0],
            dst_ref=stripes.at[0],
            send_sem=part_sem.at[0, 0, 0],
            recv_sem=part_sem.at[1, of_core, of_col],
            device_id={"col": of_col, "sub": of_core},
            device_id_type=MESH,
        )

    def extra_arrival(kind, of_core, of_col):
        lines = pl.ds(0, high)
        return pltpu.make_async_remote_copy(
            src_ref=flux.at[0, lines, :],
            dst_ref=(flux, spot)[kind].at[0, lines, :],
            send_sem=extra_sem.at[kind, 0, 0, 0],
            recv_sem=extra_sem.at[kind, 1, of_core, of_col],
            device_id={"col": of_col, "sub": of_core},
            device_id_type=MESH,
        )

    senders(lambda of_core, of_col: part_arrival(of_core, of_col).wait_recv())
    for which, _, receives in edges:

        @pl.when(receives)
        def _():
            edge_copy(which, 0, 0).wait_recv()

    top = above[:MARGIN]
    if high == MARGIN:
        top = top + second[...]
    tiles = [top]
    carry = above[MARGIN:]
    for index in range(team):
        tiles.append(stripes[index, :MARGIN] + carry)
        if high > MARGIN:
            tiles.append(stripes[index, MARGIN:high])
        carry = stripes[index, high:]
    tiles.append(below[...] + carry)
    total = jnp.concatenate(tiles, 0)
    middle = jnp.sum(total[MARGIN : MARGIN + SUBN].reshape(SUBN // 8, 8, 2 * SUBN), 0)
    lane = lax.broadcasted_iota(jnp.int32, (8, SUBN), 1)
    sums[block] = jnp.where(lane < MARGIN, middle[:, SUBN:], middle[:, :SUBN])

    def sum_copy(step):
        to = lax.rem(block + step, blocks)
        return pltpu.make_async_remote_copy(
            src_ref=sums.at[block],
            dst_ref=sums.at[block],
            send_sem=sum_sem.at[0, step],
            recv_sem=sum_sem.at[1, step],
            device_id={"row": to // cols, "col": lax.rem(to, cols)},
            device_id_type=MESH,
        )

    each(blocks, lambda step: sum_copy(step).start())

    vectors, last, rims = (
        (halves[0, lines, :lanes], halves[1, lines, :lanes])
        for lines, lanes in (
            (slice(0, SIDE), SIDE),
            (slice(SIDE, 2 * SIDE), 2 * SUBN),
            (slice(2 * SIDE, 2 * SIDE + 2 * MARGIN), SIDE),
        )
    )
    inverse = tables[2 * SIDE : 3 * SIDE, :SIDE]
    data = split_bf16(total[:, :SIDE])
    data = split_bf16(dot_three(data, vectors))
    data = dot_three(vectors, data) * inverse
    data = split_bf16(dot_three(vectors, split_bf16(data)))
    sides = dot_three(
        rims,
        (data[0][MARGIN : MARGIN + SUBN], data[1][MARGIN : MARGIN + SUBN]),
        ((1,), (1,)),
    )
    rim_out[...] = sides
    solved = dot_three(data, last)
    for index, lines in enumerate((slice(0, MARGIN), slice(SUBN + MARGIN, SIDE))):
        ends = solved[lines, SUBN:]
        row_out[index, 0] = jnp.where(lane >= SUBN - MARGIN, ends, 0.0)
        row_out[index, 1] = solved[lines, :SUBN]
        row_out[index, 2] = jnp.where(lane < MARGIN, ends, 0.0)

    moves = []
    for down in (-1, 0, 1):
        for right in (-1, 0, 1):
            if down == 0 and right == 0:
                continue
            number = (down + 1) * 3 + right + 1
            if down == 0:
                src = rim_out.at[pl.ds(MARGIN if right > 0 else 0, MARGIN)]
                dst = side_in.at[pl.ds(0 if right > 0 else SUBN - MARGIN, MARGIN)]
            else:
                src = row_out.at[(down + 1) // 2, right + 1]
                dst = row_in.at[(down + 1) // 2, right + 1]
            copy = pltpu.make_async_remote_copy(
                src_ref=src,
                dst_ref=dst,
                send_sem=fold_sem.at[0, number],
                recv_sem=fold_sem.at[1, number],
                device_id={"row": row + down, "col": col + right},
                device_id_type=MESH,
            )

            def exists(sign):
                test = row >= 0
                if down:
                    at = row + sign * down
                    test = test & (at >= 0) & (at < rows)
                if right:
                    at = col + sign * right
                    test = test & (at >= 0) & (at < cols)
                return test

            moves.append((copy, exists(1), exists(-1)))

    for copy, sends, _ in moves:
        pl.when(sends)(copy.start)

    each(blocks, lambda step: sum_copy(step).wait_recv())
    mix = sums[0] * coarse[block, 0]
    for index in range(1, blocks):
        mix = mix + sums[index] * coarse[block, index]
    lift = jnp.sum(jnp.sum(mix, 0, keepdims=True), 1, keepdims=True)
    mine = solved[MARGIN : MARGIN + SUBN, :SUBN] + lift

    for copy, _, receives in moves:
        pl.when(receives)(copy.wait_recv)
    mine = mine + side_in[...].T
    phase[0] = jnp.concatenate(
        [
            mine[:MARGIN] + row_in[1, 0] + row_in[1, 1] + row_in[1, 2],
            mine[MARGIN : SUBN - MARGIN],
            mine[SUBN - MARGIN :] + row_in[0, 0] + row_in[0, 1] + row_in[0, 2],
        ],
        0,
    )

    for kind in range(2):
        senders(lambda of_core, of_col: extra_arrival(kind, of_core, of_col).wait_recv())
    for frame in range(frames):
        members(frame, lambda across: part_copy(frame, across).wait_send())
        for kind in range(2):
            members(frame, lambda across: extra_copy(kind, frame, across).wait_send())
        for which, sends, _ in edges:

            @pl.when(sends)
            def _():
                for across in range(cols):
                    edge_copy(which, frame, across).wait_send()

    each(blocks, lambda step: sum_copy(step).wait_send())
    for copy, sends, _ in moves:
        pl.when(sends)(copy.wait_send)


def deliver(phase, flux, spot, phase_out, flux_out, spot_out, sem):
    copies = [
        pltpu.make_async_copy(near, far, sem.at[index])
        for index, (near, far) in enumerate(
            ((phase, phase_out), (flux, flux_out), (spot, spot_out))
        )
    ]
    for copy in copies:
        copy.start()
    for copy in copies:
        copy.wait()


def body(sizes, pixels):
    rows, cols, cores = sizes
    frames, pixel_rows, pixel_cols = pixels.shape
    high = pixel_rows // PIX
    wide = pixel_cols // PIX
    team = cols * cores
    blocks = rows * cols
    vmem = pl.BlockSpec(memory_space=pltpu.VMEM)
    hbm = pl.BlockSpec(memory_space=pltpu.HBM)
    square = jax.ShapeDtypeStruct((1, SUBN, SUBN), jnp.float32)
    tables = host_tables()
    coarse = coarse_inverse(rows, cols)
    constants = np.zeros((2304, 2 * SUBN), np.float32)
    constants[: tables.shape[0]] = tables
    constants[tables.shape[0] : tables.shape[0] + blocks, : coarse.shape[1]] = coarse
    dma = pltpu.SemaphoreType.DMA
    results = pl.pallas_call(
        functools.partial(kernel, sizes),
        out_shape=(square, square, square),
        in_specs=[hbm] * 2,
        out_specs=(vmem, vmem, vmem),
        scratch_shapes=[
            pltpu.VMEM((frames, pixel_rows, pixel_cols), jnp.bfloat16),
            pltpu.VMEM(tables.shape, jnp.float32),
            pltpu.VMEM((2, 2 * SIDE + 2 * MARGIN, 2 * SUBN), jnp.bfloat16),
            pltpu.SMEM(coarse.shape, jnp.float32),
            pltpu.VMEM((SUBN * PIX, SUBN), jnp.bfloat16),
            pltpu.VMEM((SUBN * PIX, 2 * SUBN), jnp.bfloat16),
            pltpu.VMEM((frames, high + MARGIN, wide + SUBN), jnp.float32),
            pltpu.VMEM((frames, 2, high, wide), jnp.float32),
            pltpu.VMEM((team, high + MARGIN, 2 * SUBN), jnp.float32),
            pltpu.VMEM((2 * MARGIN, 2 * SUBN), jnp.float32),
            pltpu.VMEM((MARGIN, 2 * SUBN), jnp.float32),
            pltpu.VMEM((MARGIN, 2 * SUBN), jnp.float32),
            pltpu.VMEM((blocks, 8, SUBN), jnp.float32),
            pltpu.VMEM((2 * MARGIN, SUBN), jnp.float32),
            pltpu.VMEM((2, 3, MARGIN, SUBN), jnp.float32),
            pltpu.VMEM((SUBN, SUBN), jnp.float32),
            pltpu.VMEM((2, 3, MARGIN, SUBN), jnp.float32),
            dma((frames, cols)),
            dma((2,)),
            dma((2, cores, cols)),
            dma((2, 2, cores, cols)),
            dma((3, 2, cores, cols)),
            dma((2, blocks)),
            dma((2, 9)),
        ],
        compiler_params=pltpu.CompilerParams(
            collective_id=0, has_side_effects=True, vmem_limit_bytes=53_000_000
        ),
        name="schwarz",
    )(pixels, constants)
    return pl.pallas_call(
        deliver,
        out_shape=(square, square, square),
        in_specs=[vmem] * 3,
        out_specs=(hbm, hbm, hbm),
        scratch_shapes=[dma((3,))],
        name="deliver",
    )(*results)


def solution(mesh):
    sizes = tuple(mesh.shape[name] for name in ("row", "col", "sub"))
    out = P(("groups", "sub"), "row", "col")
    return jax.shard_map(
        functools.partial(body, sizes),
        mesh=mesh,
        in_specs=(P("groups", ("row", "col", "sub"), None),),
        out_specs=(out, out, out),
        check_vma=False,
    )
```

```python
import functools
import math

import jax
import jax.numpy as jnp
import numpy as np
from jax import lax
from jax.experimental import pallas as pl
from jax.experimental.pallas import tpu as pltpu
from jax.sharding import PartitionSpec as P

PIX = 8
SUBN = 128
MARGIN = 8
SIDE = SUBN + 2 * MARGIN
damping = 2e-05
MESH = pl.DeviceIdType.MESH


def split_bf16(values):
    high = values.astype(jnp.bfloat16)
    return high, (values - high.astype(jnp.float32)).astype(jnp.bfloat16)


def dot(left, right, contract=((1,), (0,))):
    return lax.dot_general(left, right, (contract, ((), ())), preferred_element_type=jnp.float32)


def dot_three(left, right, contract=((1,), (0,))):
    (left_high, left_low), (right_high, right_low) = left, right
    return (
        dot(left_high, right_high, contract)
        + dot(left_low, right_high, contract)
        + dot(left_high, right_low, contract)
    )


def host_tables():
    order = np.arange(1, SIDE + 1, dtype=np.float64)
    vectors = np.sqrt(2.0 / (SIDE + 1)) * np.sin(math.pi * np.outer(order, order) / (SIDE + 1))
    spectrum = 2.0 - 2.0 * np.cos(math.pi * order / (SIDE + 1))
    inverse = 1.0 / (spectrum[:, None] + spectrum[None, :] + damping)
    corner = np.zeros((SIDE, SUBN))
    corner[:, :MARGIN] = vectors[:, SUBN + MARGIN :]
    corner[:, SUBN - MARGIN :] = vectors[:, :MARGIN]
    last = np.concatenate([vectors[:, MARGIN : MARGIN + SUBN], corner], 1)
    rims = np.concatenate([vectors[:MARGIN], vectors[SUBN + MARGIN :]], 0)
    wide = [np.pad(part, ((0, 0), (0, 2 * SUBN - part.shape[1]))) for part in (vectors, inverse, rims)]
    return np.concatenate([wide[0], last, wide[1], wide[2]], 0).astype(np.float32)


def coarse_inverse(blocks_down, blocks_across):
    number = blocks_down * blocks_across
    labels = np.arange(number)
    down, across = labels // blocks_across, labels % blocks_across
    apart = np.abs(down[:, None] - down[None, :]) + np.abs(across[:, None] - across[None, :])
    touching = (apart == 1).astype(np.float64)
    laplace = np.diag(touching.sum(1)) - touching
    matrix = SUBN * laplace + damping * SUBN * SUBN * np.eye(number)
    root = np.linalg.inv(np.linalg.cholesky(matrix))
    spare = max(SUBN - number, 0)
    return np.pad(root.T @ root, ((0, 0), (0, spare))).astype(np.float32)


def each(count, step):
    if count <= 16:
        for index in range(1, count):
            step(index)
    else:
        pl.loop(1, count)(step)


def kernel(
    sizes,
    pixels,
    constants,
    out,
    loaded,
    tables,
    halves,
    coarse,
    pick_one,
    pick_two,
    parts,
    extras,
    stripes,
    above,
    below,
    second,
    sums,
    rim_out,
    row_out,
    side_in,
    row_in,
    load_sem,
    table_sem,
    part_sem,
    extra_sem,
    edge_sem,
    sum_sem,
    fold_sem,
):
    rows, cols, cores = sizes
    frames, pixel_rows, pixel_cols = pixels.shape
    high = pixel_rows // PIX
    wide = pixel_cols // PIX
    team = cols * cores
    blocks = rows * cols
    chunk = SUBN * PIX
    row, col, core = (lax.axis_index(name) for name in ("row", "col", "sub"))
    seat = col * cores + core
    block = row * cols + col

    def load(frame, tile):
        lanes = pl.ds(tile * chunk, chunk)
        return pltpu.make_async_copy(
            pixels.at[frame, :, lanes], loaded.at[frame, :, lanes], load_sem.at[frame, tile]
        )

    for frame in range(frames):
        for tile in range(cols):
            load(frame, tile).start()
    fetches = [
        pltpu.make_async_copy(far, near, table_sem.at[index])
        for index, (far, near) in enumerate(
            (
                (constants.at[pl.ds(0, tables.shape[0])], tables),
                (
                    constants.at[
                        pl.ds(tables.shape[0], coarse.shape[0]), pl.ds(0, coarse.shape[1])
                    ],
                    coarse,
                ),
            )
        )
    ]
    for copy in fetches:
        copy.start()

    for ref in (above, below, second, side_in, row_in):
        ref[...] = jnp.zeros_like(ref)

    barrier = pltpu.get_barrier_semaphore()
    everyone = rows * team
    here = row * team + seat

    def greet(step):
        other = lax.rem(here + step, everyone)
        pl.semaphore_signal(
            barrier,
            inc=1,
            device_id={
                "row": other // team,
                "col": lax.rem(other, team) // cores,
                "sub": lax.rem(other, cores),
            },
            device_id_type=MESH,
        )

    each(everyone, greet)

    pixel = lax.broadcasted_iota(jnp.int32, (chunk, SUBN), 0)
    lane = lax.broadcasted_iota(jnp.int32, (chunk, SUBN), 1)
    inside = (pixel >> 3) == lane
    offset = (pixel & 7).astype(jnp.float32) - (PIX - 1) / 2.0
    pick_one[...] = jnp.where(inside, 1.0, 0.0).astype(jnp.bfloat16)
    pick_two[:, :SUBN] = jnp.where(inside, offset, 0.0).astype(jnp.bfloat16)
    pick_two[:, SUBN:] = jnp.where(inside, offset * offset, 0.0).astype(jnp.bfloat16)
    line = lax.broadcasted_iota(jnp.int32, (high, pixel_rows), 0)
    pixel = lax.broadcasted_iota(jnp.int32, (high, pixel_rows), 1)
    inside = (pixel >> 3) == line
    offset = (pixel & 7).astype(jnp.float32) - (PIX - 1) / 2.0
    gather = jnp.concatenate(
        [
            jnp.where(inside, 1.0, 0.0),
            jnp.where(inside, offset, 0.0),
            jnp.where(inside, offset * offset, 0.0),
        ],
        0,
    ).astype(jnp.bfloat16)

    def window(across):
        return pl.ds(pl.multiple_of(across * SUBN, SUBN), 2 * SUBN)

    def square(across):
        return pl.ds(pl.multiple_of(across * SUBN, SUBN), SUBN)

    def part_copy(frame, across):
        return pltpu.make_async_remote_copy(
            src_ref=parts.at[frame, :, window(across)],
            dst_ref=stripes.at[seat],
            send_sem=part_sem.at[0, frame, across],
            recv_sem=part_sem.at[1, core, col],
            device_id={"col": across, "sub": frame},
            device_id_type=MESH,
        )

    own_lines = pl.ds(pl.multiple_of(seat * high, 8), high)

    def extra_copy(kind, frame, across):
        return pltpu.make_async_remote_copy(
            src_ref=extras.at[frame, kind, :, square(across)],
            dst_ref=out.at[1 + kind, own_lines, :],
            send_sem=extra_sem.at[kind, 0, frame, across],
            recv_sem=extra_sem.at[kind, 1, core, col],
            device_id={"col": across, "sub": frame},
            device_id_type=MESH,
        )

    def edge_copy(which, frame, across):
        lines = (
            pl.ds(0, MARGIN),
            pl.ds(high - MARGIN, 2 * MARGIN),
            pl.ds(high, MARGIN),
        )[which]
        return pltpu.make_async_remote_copy(
            src_ref=parts.at[frame, lines, window(across)],
            dst_ref=(below, above, second)[which],
            send_sem=edge_sem.at[which, 0, frame, across],
            recv_sem=edge_sem.at[which, 1, 0, 0],
            device_id={"row": row + (-1 if which == 0 else 1), "col": across, "sub": frame},
            device_id_type=MESH,
        )

    edges = [
        (0, (seat == 0) & (row > 0), row < rows - 1),
        (1, (seat == team - 1) & (row < rows - 1), row > 0),
    ]
    if high == MARGIN:
        edges.append((2, (seat == team - 2) & (row < rows - 1), row > 0))

    def members(frame, action):
        for step in range(1, cols):
            action(lax.rem(col + step, cols))
        pl.when(core != frame)(lambda: action(col))

    def senders(action):
        def one(step):
            other = lax.rem(seat + step, team)
            action(lax.rem(other, cores), other // cores)

        each(team, one)

    line = lax.broadcasted_iota(jnp.int32, (high, wide), 0)
    column = lax.broadcasted_iota(jnp.int32, (high, wide), 1)
    stripe = row * team + seat
    for frame in range(frames):
        summed = []
        for tile in range(cols):
            load(frame, tile).wait()
            summed.append(dot(gather, loaded[frame, :, tile * chunk : (tile + 1) * chunk]))
        near, far = split_bf16(
            jnp.concatenate(
                [part[kind * high : (kind + 1) * high] for kind in range(3) for part in summed], 0
            )
        )
        tall = cols * high
        ones = dot(near, pick_one[...]) + dot(far, pick_one[...])
        twos = dot(near[:tall], pick_two[...]) + dot(far[:tall], pick_two[...])
        intensity = ones[:tall]
        scale = 1.0 / intensity
        slope_x = twos[:, :SUBN] * scale
        slope_y = ones[tall : 2 * tall] * scale
        moment_two = twos[:, SUBN:] + ones[2 * tall :]

        def grid(values):
            return jnp.concatenate(
                [values[tile * high : (tile + 1) * high] for tile in range(cols)], 1
            )

        flow_x = jnp.where(column < wide - 1, grid(slope_x), 0.0)
        flow_y = jnp.where(stripe * high + line < rows * SUBN - 1, grid(slope_y), 0.0)
        over = pltpu.roll(flow_y, 1, 0)
        source = pltpu.roll(flow_x, 1, 1) - flow_x - flow_y + jnp.where(line > 0, over, 0.0)
        carried = jnp.where(line == 0, over, 0.0)[:MARGIN]
        both = jnp.concatenate([source, carried], 0)
        both = jnp.concatenate([both, jnp.zeros((high + MARGIN, SUBN), jnp.float32)], 1)
        parts[frame] = pltpu.roll(both, MARGIN, 1)
        if frame == 0:
            pl.semaphore_wait(barrier, everyone - 1)
        members(frame, lambda across: part_copy(frame, across).start())
        for which, sends, _ in edges:

            @pl.when(sends)
            def _():
                for across in range(cols):
                    edge_copy(which, frame, across).start()

        extras[frame, 0] = grid(intensity) * (1.0 / (PIX * PIX))
        extras[frame, 1] = grid(moment_two * scale - slope_x * slope_x - slope_y * slope_y)

    for frame in range(frames):
        for kind in range(2):
            members(frame, lambda across: extra_copy(kind, frame, across).start())

    for copy in fetches:
        copy.wait()
    for lines, source_lines in (
        (slice(0, 2 * SIDE), slice(0, 2 * SIDE)),
        (slice(2 * SIDE, 2 * SIDE + 2 * MARGIN), slice(3 * SIDE, 3 * SIDE + 2 * MARGIN)),
    ):
        halves[0, lines], halves[1, lines] = split_bf16(tables[source_lines])

    stripes[seat] = parts[core, :, window(col)]
    out[1, own_lines, :] = extras[core, 0, :, square(col)]
    out[2, own_lines, :] = extras[core, 1, :, square(col)]

    def part_arrival(of_core, of_col):
        return pltpu.make_async_remote_copy(
            src_ref=stripes.at[0],
            dst_ref=stripes.at[0],
            send_sem=part_sem.at[0, 0, 0],
            recv_sem=part_sem.at[1, of_core, of_col],
            device_id={"col": of_col, "sub": of_core},
            device_id_type=MESH,
        )

    def extra_arrival(kind, of_core, of_col):
        lines = pl.ds(0, high)
        return pltpu.make_async_remote_copy(
            src_ref=out.at[1 + kind, lines, :],
            dst_ref=out.at[1 + kind, lines, :],
            send_sem=extra_sem.at[kind, 0, 0, 0],
            recv_sem=extra_sem.at[kind, 1, of_core, of_col],
            device_id={"col": of_col, "sub": of_core},
            device_id_type=MESH,
        )

    senders(lambda of_core, of_col: part_arrival(of_core, of_col).wait_recv())
    for which, _, receives in edges:

        @pl.when(receives)
        def _():
            edge_copy(which, 0, 0).wait_recv()

    top = above[:MARGIN]
    if high == MARGIN:
        top = top + second[...]
    tiles = [top]
    carry = above[MARGIN:]
    for index in range(team):
        tiles.append(stripes[index, :MARGIN] + carry)
        if high > MARGIN:
            tiles.append(stripes[index, MARGIN:high])
        carry = stripes[index, high:]
    tiles.append(below[...] + carry)
    total = jnp.concatenate(tiles, 0)
    middle = jnp.sum(total[MARGIN : MARGIN + SUBN].reshape(SUBN // 8, 8, 2 * SUBN), 0)
    lane = lax.broadcasted_iota(jnp.int32, (8, SUBN), 1)
    sums[block] = jnp.where(lane < MARGIN, middle[:, SUBN:], middle[:, :SUBN])

    def sum_copy(step):
        to = lax.rem(block + step, blocks)
        return pltpu.make_async_remote_copy(
            src_ref=sums.at[block],
            dst_ref=sums.at[block],
            send_sem=sum_sem.at[0, step],
            recv_sem=sum_sem.at[1, step],
            device_id={"row": to // cols, "col": lax.rem(to, cols)},
            device_id_type=MESH,
        )

    each(blocks, lambda step: sum_copy(step).start())

    vectors, last, rims = (
        (halves[0, lines, :lanes], halves[1, lines, :lanes])
        for lines, lanes in (
            (slice(0, SIDE), SIDE),
            (slice(SIDE, 2 * SIDE), 2 * SUBN),
            (slice(2 * SIDE, 2 * SIDE + 2 * MARGIN), SIDE),
        )
    )
    inverse = tables[2 * SIDE : 3 * SIDE, :SIDE]
    data = split_bf16(total[:, :SIDE])
    data = split_bf16(dot_three(data, vectors))
    data = dot_three(vectors, data) * inverse
    data = split_bf16(dot_three(vectors, split_bf16(data)))
    sides = dot_three(
        rims,
        (data[0][MARGIN : MARGIN + SUBN], data[1][MARGIN : MARGIN + SUBN]),
        ((1,), (1,)),
    )
    rim_out[...] = sides
    solved = dot_three(data, last)
    for index, lines in enumerate((slice(0, MARGIN), slice(SUBN + MARGIN, SIDE))):
        ends = solved[lines, SUBN:]
        row_out[index, 0] = jnp.where(lane >= SUBN - MARGIN, ends, 0.0)
        row_out[index, 1] = solved[lines, :SUBN]
        row_out[index, 2] = jnp.where(lane < MARGIN, ends, 0.0)

    moves = []
    for down in (-1, 0, 1):
        for right in (-1, 0, 1):
            if down == 0 and right == 0:
                continue
            number = (down + 1) * 3 + right + 1
            if down == 0:
                src = rim_out.at[pl.ds(MARGIN if right > 0 else 0, MARGIN)]
                dst = side_in.at[pl.ds(0 if right > 0 else SUBN - MARGIN, MARGIN)]
            else:
                src = row_out.at[(down + 1) // 2, right + 1]
                dst = row_in.at[(down + 1) // 2, right + 1]
            copy = pltpu.make_async_remote_copy(
                src_ref=src,
                dst_ref=dst,
                send_sem=fold_sem.at[0, number],
                recv_sem=fold_sem.at[1, number],
                device_id={"row": row + down, "col": col + right},
                device_id_type=MESH,
            )

            def exists(sign):
                test = row >= 0
                if down:
                    at = row + sign * down
                    test = test & (at >= 0) & (at < rows)
                if right:
                    at = col + sign * right
                    test = test & (at >= 0) & (at < cols)
                return test

            moves.append((copy, exists(1), exists(-1)))

    for copy, sends, _ in moves:
        pl.when(sends)(copy.start)

    each(blocks, lambda step: sum_copy(step).wait_recv())
    mix = sums[0] * coarse[block, 0]
    for index in range(1, blocks):
        mix = mix + sums[index] * coarse[block, index]
    lift = jnp.sum(jnp.sum(mix, 0, keepdims=True), 1, keepdims=True)
    mine = solved[MARGIN : MARGIN + SUBN, :SUBN] + lift

    for copy, _, receives in moves:
        pl.when(receives)(copy.wait_recv)
    mine = mine + side_in[...].T
    out[0] = jnp.concatenate(
        [
            mine[:MARGIN] + row_in[1, 0] + row_in[1, 1] + row_in[1, 2],
            mine[MARGIN : SUBN - MARGIN],
            mine[SUBN - MARGIN :] + row_in[0, 0] + row_in[0, 1] + row_in[0, 2],
        ],
        0,
    )

    for kind in range(2):
        senders(lambda of_core, of_col: extra_arrival(kind, of_core, of_col).wait_recv())
    for frame in range(frames):
        members(frame, lambda across: part_copy(frame, across).wait_send())
        for kind in range(2):
            members(frame, lambda across: extra_copy(kind, frame, across).wait_send())
        for which, sends, _ in edges:

            @pl.when(sends)
            def _():
                for across in range(cols):
                    edge_copy(which, frame, across).wait_send()

    each(blocks, lambda step: sum_copy(step).wait_send())
    for copy, sends, _ in moves:
        pl.when(sends)(copy.wait_send)


def body(sizes, pixels):
    rows, cols, cores = sizes
    frames, pixel_rows, pixel_cols = pixels.shape
    high = pixel_rows // PIX
    wide = pixel_cols // PIX
    team = cols * cores
    blocks = rows * cols
    vmem = pl.BlockSpec(memory_space=pltpu.VMEM)
    hbm = pl.BlockSpec(memory_space=pltpu.HBM)
    tables = host_tables()
    coarse = coarse_inverse(rows, cols)
    constants = np.zeros((2304, 2 * SUBN), np.float32)
    constants[: tables.shape[0]] = tables
    constants[tables.shape[0] : tables.shape[0] + blocks, : coarse.shape[1]] = coarse
    dma = pltpu.SemaphoreType.DMA
    results = pl.pallas_call(
        functools.partial(kernel, sizes),
        out_shape=jax.ShapeDtypeStruct((3, SUBN, SUBN), jnp.float32),
        in_specs=[hbm] * 2,
        out_specs=vmem,
        scratch_shapes=[
            pltpu.VMEM((frames, pixel_rows, pixel_cols), jnp.bfloat16),
            pltpu.VMEM(tables.shape, jnp.float32),
            pltpu.VMEM((2, 2 * SIDE + 2 * MARGIN, 2 * SUBN), jnp.bfloat16),
            pltpu.SMEM(coarse.shape, jnp.float32),
            pltpu.VMEM((SUBN * PIX, SUBN), jnp.bfloat16),
            pltpu.VMEM((SUBN * PIX, 2 * SUBN), jnp.bfloat16),
            pltpu.VMEM((frames, high + MARGIN, wide + SUBN), jnp.float32),
            pltpu.VMEM((frames, 2, high, wide), jnp.float32),
            pltpu.VMEM((team, high + MARGIN, 2 * SUBN), jnp.float32),
            pltpu.VMEM((2 * MARGIN, 2 * SUBN), jnp.float32),
            pltpu.VMEM((MARGIN, 2 * SUBN), jnp.float32),
            pltpu.VMEM((MARGIN, 2 * SUBN), jnp.float32),
            pltpu.VMEM((blocks, 8, SUBN), jnp.float32),
            pltpu.VMEM((2 * MARGIN, SUBN), jnp.float32),
            pltpu.VMEM((2, 3, MARGIN, SUBN), jnp.float32),
            pltpu.VMEM((SUBN, SUBN), jnp.float32),
            pltpu.VMEM((2, 3, MARGIN, SUBN), jnp.float32),
            dma((frames, cols)),
            dma((2,)),
            dma((2, cores, cols)),
            dma((2, 2, cores, cols)),
            dma((3, 2, cores, cols)),
            dma((2, blocks)),
            dma((2, 9)),
        ],
        compiler_params=pltpu.CompilerParams(
            collective_id=0, has_side_effects=True, vmem_limit_bytes=53 * 1024 * 1024
        ),
        name="schwarz",
    )(pixels, constants)
    return tuple(results[index : index + 1] for index in range(3))


def solution(mesh):
    sizes = tuple(mesh.shape[name] for name in ("row", "col", "sub"))
    out = P(("groups", "sub"), "row", "col")
    return jax.shard_map(
        functools.partial(body, sizes),
        mesh=mesh,
        in_specs=(P("groups", ("row", "col", "sub"), None),),
        out_specs=(out, out, out),
        check_vma=False,
    )
```

```python
import functools
import math

import jax
import jax.numpy as jnp
import numpy as np
from jax import lax
from jax.experimental import pallas as pl
from jax.experimental.pallas import tpu as pltpu
from jax.sharding import PartitionSpec as P

PIX = 8
SUBN = 128
MARGIN = 8
SIDE = SUBN + 2 * MARGIN
damping = 2e-05
MESH = pl.DeviceIdType.MESH


def split_bf16(values):
    high = values.astype(jnp.bfloat16)
    return high, (values - high.astype(jnp.float32)).astype(jnp.bfloat16)


def dot(left, right, contract=((1,), (0,))):
    return lax.dot_general(left, right, (contract, ((), ())), preferred_element_type=jnp.float32)


def dot_three(left, right, contract=((1,), (0,))):
    (left_high, left_low), (right_high, right_low) = left, right
    return (
        dot(left_high, right_high, contract)
        + dot(left_low, right_high, contract)
        + dot(left_high, right_low, contract)
    )


def host_tables():
    order = np.arange(1, SIDE + 1, dtype=np.float64)
    vectors = np.sqrt(2.0 / (SIDE + 1)) * np.sin(math.pi * np.outer(order, order) / (SIDE + 1))
    spectrum = 2.0 - 2.0 * np.cos(math.pi * order / (SIDE + 1))
    inverse = 1.0 / (spectrum[:, None] + spectrum[None, :] + damping)
    corner = np.zeros((SIDE, SUBN))
    corner[:, :MARGIN] = vectors[:, SUBN + MARGIN :]
    corner[:, SUBN - MARGIN :] = vectors[:, :MARGIN]
    last = np.concatenate([vectors[:, MARGIN : MARGIN + SUBN], corner], 1)
    rims = np.concatenate([vectors[:MARGIN], vectors[SUBN + MARGIN :]], 0)
    wide = [np.pad(part, ((0, 0), (0, 2 * SUBN - part.shape[1]))) for part in (vectors, inverse, rims)]
    return np.concatenate([wide[0], last, wide[1], wide[2]], 0).astype(np.float32)


def coarse_inverse(blocks_down, blocks_across):
    number = blocks_down * blocks_across
    labels = np.arange(number)
    down, across = labels // blocks_across, labels % blocks_across
    apart = np.abs(down[:, None] - down[None, :]) + np.abs(across[:, None] - across[None, :])
    touching = (apart == 1).astype(np.float64)
    laplace = np.diag(touching.sum(1)) - touching
    matrix = SUBN * laplace + damping * SUBN * SUBN * np.eye(number)
    root = np.linalg.inv(np.linalg.cholesky(matrix))
    spare = max(SUBN - number, 0)
    return np.pad(root.T @ root, ((0, 0), (0, spare))).astype(np.float32)


def each(count, step):
    if count <= 16:
        for index in range(1, count):
            step(index)
    else:
        pl.loop(1, count)(step)


def kernel(
    sizes,
    pixels,
    constants,
    out,
    loaded,
    tables,
    halves,
    coarse,
    pick_one,
    pick_two,
    parts,
    extras,
    stripes,
    above,
    below,
    second,
    sums,
    rim_out,
    row_out,
    side_in,
    row_in,
    load_sem,
    table_sem,
    part_sem,
    extra_sem,
    edge_sem,
    sum_sem,
    fold_sem,
):
    rows, cols, cores = sizes
    frames, pixel_rows, pixel_cols = pixels.shape
    high = pixel_rows // PIX
    wide = pixel_cols // PIX
    team = cols * cores
    blocks = rows * cols
    chunk = SUBN * PIX
    row, col, core = (lax.axis_index(name) for name in ("row", "col", "sub"))
    seat = col * cores + core
    block = row * cols + col

    def load(frame, tile):
        lanes = pl.ds(tile * chunk, chunk)
        return pltpu.make_async_copy(
            pixels.at[frame, :, lanes], loaded.at[frame, :, lanes], load_sem.at[frame, tile]
        )

    for frame in range(frames):
        for tile in range(cols):
            load(frame, tile).start()
    fetches = [
        pltpu.make_async_copy(far, near, table_sem.at[index])
        for index, (far, near) in enumerate(
            (
                (constants.at[pl.ds(0, tables.shape[0])], tables),
                (
                    constants.at[
                        pl.ds(tables.shape[0], coarse.shape[0]), pl.ds(0, coarse.shape[1])
                    ],
                    coarse,
                ),
            )
        )
    ]
    for copy in fetches:
        copy.start()

    for ref in (above, below, second, side_in, row_in):
        ref[...] = jnp.zeros_like(ref)

    barrier = pltpu.get_barrier_semaphore()
    everyone = rows * team
    here = row * team + seat

    def greet(step):
        other = lax.rem(here + step, everyone)
        pl.semaphore_signal(
            barrier,
            inc=1,
            device_id={
                "row": other // team,
                "col": lax.rem(other, team) // cores,
                "sub": lax.rem(other, cores),
            },
            device_id_type=MESH,
        )

    each(everyone, greet)

    pixel = lax.broadcasted_iota(jnp.int32, (chunk, SUBN), 0)
    lane = lax.broadcasted_iota(jnp.int32, (chunk, SUBN), 1)
    inside = (pixel >> 3) == lane
    offset = (pixel & 7).astype(jnp.float32) - (PIX - 1) / 2.0
    pick_one[...] = jnp.where(inside, 1.0, 0.0).astype(jnp.bfloat16)
    pick_two[:, :SUBN] = jnp.where(inside, offset, 0.0).astype(jnp.bfloat16)
    pick_two[:, SUBN:] = jnp.where(inside, offset * offset, 0.0).astype(jnp.bfloat16)
    line = lax.broadcasted_iota(jnp.int32, (high, pixel_rows), 0)
    pixel = lax.broadcasted_iota(jnp.int32, (high, pixel_rows), 1)
    inside = (pixel >> 3) == line
    offset = (pixel & 7).astype(jnp.float32) - (PIX - 1) / 2.0
    gather = jnp.concatenate(
        [
            jnp.where(inside, 1.0, 0.0),
            jnp.where(inside, offset, 0.0),
            jnp.where(inside, offset * offset, 0.0),
        ],
        0,
    ).astype(jnp.bfloat16)

    def square(across):
        return pl.ds(pl.multiple_of(across * SUBN, SUBN), SUBN)

    def part_copy(frame, across):
        return pltpu.make_async_remote_copy(
            src_ref=parts.at[frame, across, pl.ds(0, high + 2 * MARGIN)],
            dst_ref=stripes.at[seat],
            send_sem=part_sem.at[0, frame, across],
            recv_sem=part_sem.at[1, core, col],
            device_id={"col": across, "sub": frame},
            device_id_type=MESH,
        )

    own_lines = pl.ds(pl.multiple_of(seat * high, 8), high)

    def extra_copy(kind, frame, across):
        return pltpu.make_async_remote_copy(
            src_ref=extras.at[frame, kind, :, square(across)],
            dst_ref=out.at[1 + kind, own_lines, :],
            send_sem=extra_sem.at[kind, 0, frame, across],
            recv_sem=extra_sem.at[kind, 1, core, col],
            device_id={"col": across, "sub": frame},
            device_id_type=MESH,
        )

    def edge_copy(which, frame, across):
        lines = (
            pl.ds(0, 2 * MARGIN),
            pl.ds(high, 3 * MARGIN),
            pl.ds(high + MARGIN, 2 * MARGIN),
        )[which]
        return pltpu.make_async_remote_copy(
            src_ref=parts.at[frame, across, lines],
            dst_ref=(below, above, second)[which],
            send_sem=edge_sem.at[which, 0, frame, across],
            recv_sem=edge_sem.at[which, 1, 0, 0],
            device_id={"row": row + (-1 if which == 0 else 1), "col": across, "sub": frame},
            device_id_type=MESH,
        )

    edges = [
        (0, (seat == 0) & (row > 0), row < rows - 1),
        (1, (seat == team - 1) & (row < rows - 1), row > 0),
    ]
    if high == MARGIN:
        edges.append((2, (seat == team - 2) & (row < rows - 1), row > 0))

    def members(frame, action):
        for step in range(1, cols):
            action(lax.rem(col + step, cols))
        pl.when(core != frame)(lambda: action(col))

    def senders(action):
        def one(step):
            other = lax.rem(seat + step, team)
            action(lax.rem(other, cores), other // cores)

        each(team, one)

    line = lax.broadcasted_iota(jnp.int32, (high, wide), 0)
    column = lax.broadcasted_iota(jnp.int32, (high, wide), 1)
    stripe = row * team + seat
    lane8 = lax.broadcasted_iota(jnp.int32, (MARGIN, SUBN), 1)
    for frame in range(frames):
        summed = []
        for tile in range(cols):
            load(frame, tile).wait()
            summed.append(dot(gather, loaded[frame, :, tile * chunk : (tile + 1) * chunk]))
        near, far = split_bf16(
            jnp.concatenate(
                [part[kind * high : (kind + 1) * high] for kind in range(3) for part in summed], 0
            )
        )
        tall = cols * high
        ones = dot(near, pick_one[...]) + dot(far, pick_one[...])
        twos = dot(near[:tall], pick_two[...]) + dot(far[:tall], pick_two[...])
        intensity = ones[:tall]
        scale = 1.0 / intensity
        slope_x = twos[:, :SUBN] * scale
        slope_y = ones[tall : 2 * tall] * scale
        moment_two = twos[:, SUBN:] + ones[2 * tall :]

        def grid(values):
            return jnp.concatenate(
                [values[tile * high : (tile + 1) * high] for tile in range(cols)], 1
            )

        flow_x = jnp.where(column < wide - 1, grid(slope_x), 0.0)
        flow_y = jnp.where(stripe * high + line < rows * SUBN - 1, grid(slope_y), 0.0)
        over = pltpu.roll(flow_y, 1, 0)
        source = pltpu.roll(flow_x, 1, 1) - flow_x - flow_y + jnp.where(line > 0, over, 0.0)
        carried = jnp.where(line == 0, over, 0.0)[:MARGIN]
        both = jnp.concatenate([source, carried], 0)
        both = jnp.concatenate([both, jnp.zeros((high + MARGIN, SUBN), jnp.float32)], 1)
        both = pltpu.roll(both, MARGIN, 1)
        for across in range(cols):
            packed = jnp.zeros((MARGIN, SUBN), jnp.float32)
            for group in range(high // MARGIN + 1):
                rest = both[
                    group * MARGIN : (group + 1) * MARGIN,
                    (across + 1) * SUBN : (across + 2) * SUBN,
                ]
                rest = jnp.where(lane8 < 2 * MARGIN, rest, 0.0)
                packed = packed + (pltpu.roll(rest, 2 * MARGIN * group, 1) if group else rest)
            parts[frame, across] = jnp.concatenate(
                [packed, both[:, across * SUBN : (across + 1) * SUBN], packed], 0
            )
        extras[frame, 0] = grid(intensity) * (1.0 / (PIX * PIX))
        extras[frame, 1] = grid(moment_two * scale - slope_x * slope_x - slope_y * slope_y)

    pl.semaphore_wait(barrier, everyone - 1)
    for frame in range(frames):
        members(frame, lambda across: part_copy(frame, across).start())
    for which, sends, _ in edges:

        @pl.when(sends)
        def _():
            for frame in range(frames):
                for across in range(cols):
                    edge_copy(which, frame, across).start()

    for frame in range(frames):
        for kind in range(2):
            members(frame, lambda across: extra_copy(kind, frame, across).start())

    for copy in fetches:
        copy.wait()
    for lines, source_lines in (
        (slice(0, 2 * SIDE), slice(0, 2 * SIDE)),
        (slice(2 * SIDE, 2 * SIDE + 2 * MARGIN), slice(3 * SIDE, 3 * SIDE + 2 * MARGIN)),
    ):
        halves[0, lines], halves[1, lines] = split_bf16(tables[source_lines])

    stripes[seat] = parts[core, col, : high + 2 * MARGIN]
    out[1, own_lines, :] = extras[core, 0, :, square(col)]
    out[2, own_lines, :] = extras[core, 1, :, square(col)]

    def part_arrival(of_core, of_col):
        return pltpu.make_async_remote_copy(
            src_ref=stripes.at[0],
            dst_ref=stripes.at[0],
            send_sem=part_sem.at[0, 0, 0],
            recv_sem=part_sem.at[1, of_core, of_col],
            device_id={"col": of_col, "sub": of_core},
            device_id_type=MESH,
        )

    def extra_arrival(kind, of_core, of_col):
        lines = pl.ds(0, high)
        return pltpu.make_async_remote_copy(
            src_ref=out.at[1 + kind, lines, :],
            dst_ref=out.at[1 + kind, lines, :],
            send_sem=extra_sem.at[kind, 0, 0, 0],
            recv_sem=extra_sem.at[kind, 1, of_core, of_col],
            device_id={"col": of_col, "sub": of_core},
            device_id_type=MESH,
        )

    senders(lambda of_core, of_col: part_arrival(of_core, of_col).wait_recv())
    for which, _, receives in edges:

        @pl.when(receives)
        def _():
            edge_copy(which, 0, 0).wait_recv()

    groups = high // MARGIN

    def widen(values, packed, group):
        rest = pltpu.roll(packed, SUBN - 2 * MARGIN * group, 1) if group else packed
        return jnp.concatenate([values, rest], 1)

    top = widen(above[:MARGIN], above[2 * MARGIN :], groups - 1)
    if groups == 1:
        top = top + widen(second[:MARGIN], second[MARGIN:], groups)
    tiles = [top]
    carry = widen(above[MARGIN : 2 * MARGIN], above[2 * MARGIN :], groups)
    for index in range(team):
        packed = stripes[index, :MARGIN]
        for group in range(groups):
            lines = stripes[index, (group + 1) * MARGIN : (group + 2) * MARGIN]
            tile = widen(lines, packed, group)
            tiles.append(tile if group else tile + carry)
        carry = widen(stripes[index, high + MARGIN :], packed, groups)
    tiles.append(widen(below[MARGIN:], below[:MARGIN], 0) + carry)
    total = jnp.concatenate(tiles, 0)
    middle = jnp.sum(total[MARGIN : MARGIN + SUBN].reshape(SUBN // 8, 8, 2 * SUBN), 0)
    lane = lane8
    sums[block] = jnp.where(lane < MARGIN, middle[:, SUBN:], middle[:, :SUBN])

    def sum_copy(step):
        to = lax.rem(block + step, blocks)
        return pltpu.make_async_remote_copy(
            src_ref=sums.at[block],
            dst_ref=sums.at[block],
            send_sem=sum_sem.at[0, step],
            recv_sem=sum_sem.at[1, step],
            device_id={"row": to // cols, "col": lax.rem(to, cols)},
            device_id_type=MESH,
        )

    each(blocks, lambda step: sum_copy(step).start())

    vectors, last, rims = (
        (halves[0, lines, :lanes], halves[1, lines, :lanes])
        for lines, lanes in (
            (slice(0, SIDE), SIDE),
            (slice(SIDE, 2 * SIDE), 2 * SUBN),
            (slice(2 * SIDE, 2 * SIDE + 2 * MARGIN), SIDE),
        )
    )
    inverse = tables[2 * SIDE : 3 * SIDE, :SIDE]
    data = split_bf16(total[:, :SIDE])
    data = split_bf16(dot_three(data, vectors))
    data = dot_three(vectors, data) * inverse
    data = split_bf16(dot_three(vectors, split_bf16(data)))
    sides = dot_three(
        rims,
        (data[0][MARGIN : MARGIN + SUBN], data[1][MARGIN : MARGIN + SUBN]),
        ((1,), (1,)),
    )
    rim_out[...] = sides
    solved = dot_three(data, last)
    for index, lines in enumerate((slice(0, MARGIN), slice(SUBN + MARGIN, SIDE))):
        ends = solved[lines, SUBN:]
        row_out[index, 0] = jnp.where(lane >= SUBN - MARGIN, ends, 0.0)
        row_out[index, 1] = solved[lines, :SUBN]
        row_out[index, 2] = jnp.where(lane < MARGIN, ends, 0.0)

    moves = []
    for down in (-1, 0, 1):
        for right in (-1, 0, 1):
            if down == 0 and right == 0:
                continue
            number = (down + 1) * 3 + right + 1
            if down == 0:
                src = rim_out.at[pl.ds(MARGIN if right > 0 else 0, MARGIN)]
                dst = side_in.at[pl.ds(0 if right > 0 else SUBN - MARGIN, MARGIN)]
            else:
                src = row_out.at[(down + 1) // 2, right + 1]
                dst = row_in.at[(down + 1) // 2, right + 1]
            copy = pltpu.make_async_remote_copy(
                src_ref=src,
                dst_ref=dst,
                send_sem=fold_sem.at[0, number],
                recv_sem=fold_sem.at[1, number],
                device_id={"row": row + down, "col": col + right},
                device_id_type=MESH,
            )

            def exists(sign):
                test = row >= 0
                if down:
                    at = row + sign * down
                    test = test & (at >= 0) & (at < rows)
                if right:
                    at = col + sign * right
                    test = test & (at >= 0) & (at < cols)
                return test

            moves.append((copy, exists(1), exists(-1)))

    for copy, sends, _ in moves:
        pl.when(sends)(copy.start)

    each(blocks, lambda step: sum_copy(step).wait_recv())
    mix = sums[0] * coarse[block, 0]
    for index in range(1, blocks):
        mix = mix + sums[index] * coarse[block, index]
    lift = jnp.sum(jnp.sum(mix, 0, keepdims=True), 1, keepdims=True)
    mine = solved[MARGIN : MARGIN + SUBN, :SUBN] + lift

    for copy, _, receives in moves:
        pl.when(receives)(copy.wait_recv)
    mine = mine + side_in[...].T
    out[0] = jnp.concatenate(
        [
            mine[:MARGIN] + row_in[1, 0] + row_in[1, 1] + row_in[1, 2],
            mine[MARGIN : SUBN - MARGIN],
            mine[SUBN - MARGIN :] + row_in[0, 0] + row_in[0, 1] + row_in[0, 2],
        ],
        0,
    )

    for kind in range(2):
        senders(lambda of_core, of_col: extra_arrival(kind, of_core, of_col).wait_recv())
    for frame in range(frames):
        members(frame, lambda across: part_copy(frame, across).wait_send())
        for kind in range(2):
            members(frame, lambda across: extra_copy(kind, frame, across).wait_send())
        for which, sends, _ in edges:

            @pl.when(sends)
            def _():
                for across in range(cols):
                    edge_copy(which, frame, across).wait_send()

    each(blocks, lambda step: sum_copy(step).wait_send())
    for copy, sends, _ in moves:
        pl.when(sends)(copy.wait_send)


def body(sizes, pixels):
    rows, cols, cores = sizes
    frames, pixel_rows, pixel_cols = pixels.shape
    high = pixel_rows // PIX
    wide = pixel_cols // PIX
    team = cols * cores
    blocks = rows * cols
    vmem = pl.BlockSpec(memory_space=pltpu.VMEM)
    hbm = pl.BlockSpec(memory_space=pltpu.HBM)
    tables = host_tables()
    coarse = coarse_inverse(rows, cols)
    constants = np.zeros((2304, 2 * SUBN), np.float32)
    constants[: tables.shape[0]] = tables
    constants[tables.shape[0] : tables.shape[0] + blocks, : coarse.shape[1]] = coarse
    dma = pltpu.SemaphoreType.DMA
    results = pl.pallas_call(
        functools.partial(kernel, sizes),
        out_shape=jax.ShapeDtypeStruct((3, SUBN, SUBN), jnp.float32),
        in_specs=[hbm] * 2,
        out_specs=vmem,
        scratch_shapes=[
            pltpu.VMEM((frames, pixel_rows, pixel_cols), jnp.bfloat16),
            pltpu.VMEM(tables.shape, jnp.float32),
            pltpu.VMEM((2, 2 * SIDE + 2 * MARGIN, 2 * SUBN), jnp.bfloat16),
            pltpu.SMEM(coarse.shape, jnp.float32),
            pltpu.VMEM((SUBN * PIX, SUBN), jnp.bfloat16),
            pltpu.VMEM((SUBN * PIX, 2 * SUBN), jnp.bfloat16),
            pltpu.VMEM((frames, cols, high + 3 * MARGIN, SUBN), jnp.float32),
            pltpu.VMEM((frames, 2, high, wide), jnp.float32),
            pltpu.VMEM((team, high + 2 * MARGIN, SUBN), jnp.float32),
            pltpu.VMEM((3 * MARGIN, SUBN), jnp.float32),
            pltpu.VMEM((2 * MARGIN, SUBN), jnp.float32),
            pltpu.VMEM((2 * MARGIN, SUBN), jnp.float32),
            pltpu.VMEM((blocks, 8, SUBN), jnp.float32),
            pltpu.VMEM((2 * MARGIN, SUBN), jnp.float32),
            pltpu.VMEM((2, 3, MARGIN, SUBN), jnp.float32),
            pltpu.VMEM((SUBN, SUBN), jnp.float32),
            pltpu.VMEM((2, 3, MARGIN, SUBN), jnp.float32),
            dma((frames, cols)),
            dma((2,)),
            dma((2, cores, cols)),
            dma((2, 2, cores, cols)),
            dma((3, 2, cores, cols)),
            dma((2, blocks)),
            dma((2, 9)),
        ],
        compiler_params=pltpu.CompilerParams(
            collective_id=0, has_side_effects=True, vmem_limit_bytes=53 * 1024 * 1024
        ),
        name="schwarz",
    )(pixels, constants)
    return tuple(results[index : index + 1] for index in range(3))


def solution(mesh):
    sizes = tuple(mesh.shape[name] for name in ("row", "col", "sub"))
    out = P(("groups", "sub"), "row", "col")
    return jax.shard_map(
        functools.partial(body, sizes),
        mesh=mesh,
        in_specs=(P("groups", ("row", "col", "sub"), None),),
        out_specs=(out, out, out),
        check_vma=False,
    )
```

```python
import functools
import math

import jax
import jax.numpy as jnp
import numpy as np
from jax import lax
from jax.experimental import pallas as pl
from jax.experimental.pallas import tpu as pltpu
from jax.sharding import PartitionSpec as P

PIX = 8
SUBN = 128
MARGIN = 8
SIDE = SUBN + 2 * MARGIN
damping = 2e-05
MESH = pl.DeviceIdType.MESH


def split_bf16(values):
    high = values.astype(jnp.bfloat16)
    return high, (values - high.astype(jnp.float32)).astype(jnp.bfloat16)


def dot(left, right, contract=((1,), (0,))):
    return lax.dot_general(left, right, (contract, ((), ())), preferred_element_type=jnp.float32)


def dot_three(left, right, contract=((1,), (0,))):
    (left_high, left_low), (right_high, right_low) = left, right
    count = left_high.shape[0]
    stacked = dot(jnp.concatenate([left_high, left_low], 0), right_high, contract)
    return stacked[:count] + stacked[count:] + dot(left_high, right_low, contract)


def host_tables():
    order = np.arange(1, SIDE + 1, dtype=np.float64)
    vectors = np.sqrt(2.0 / (SIDE + 1)) * np.sin(math.pi * np.outer(order, order) / (SIDE + 1))
    spectrum = 2.0 - 2.0 * np.cos(math.pi * order / (SIDE + 1))
    inverse = 1.0 / (spectrum[:, None] + spectrum[None, :] + damping)
    corner = np.zeros((SIDE, SUBN))
    corner[:, :MARGIN] = vectors[:, SUBN + MARGIN :]
    corner[:, SUBN - MARGIN :] = vectors[:, :MARGIN]
    last = np.concatenate([vectors[:, MARGIN : MARGIN + SUBN], corner], 1)
    rims = np.concatenate([vectors[:MARGIN], vectors[SUBN + MARGIN :]], 0)
    wide = [np.pad(part, ((0, 0), (0, 2 * SUBN - part.shape[1]))) for part in (vectors, inverse, rims)]
    return np.concatenate([wide[0], last, wide[1], wide[2]], 0).astype(np.float32)


def coarse_inverse(blocks_down, blocks_across):
    number = blocks_down * blocks_across
    labels = np.arange(number)
    down, across = labels // blocks_across, labels % blocks_across
    apart = np.abs(down[:, None] - down[None, :]) + np.abs(across[:, None] - across[None, :])
    touching = (apart == 1).astype(np.float64)
    laplace = np.diag(touching.sum(1)) - touching
    matrix = SUBN * laplace + damping * SUBN * SUBN * np.eye(number)
    root = np.linalg.inv(np.linalg.cholesky(matrix))
    spare = max(SUBN - number, 0)
    return np.pad(root.T @ root, ((0, 0), (0, spare))).astype(np.float32)


def each(count, step):
    if count <= 16:
        for index in range(1, count):
            step(index)
    else:
        pl.loop(1, count)(step)


def kernel(
    sizes,
    pixels,
    constants,
    out,
    loaded,
    tables,
    halves,
    coarse,
    pick_one,
    pick_two,
    parts,
    extras,
    stripes,
    above,
    below,
    second,
    sums,
    rim_out,
    row_out,
    side_in,
    row_in,
    load_sem,
    table_sem,
    part_sem,
    extra_sem,
    edge_sem,
    sum_sem,
    fold_sem,
):
    rows, cols, cores = sizes
    frames, pixel_rows, pixel_cols = pixels.shape
    high = pixel_rows // PIX
    wide = pixel_cols // PIX
    team = cols * cores
    blocks = rows * cols
    chunk = SUBN * PIX
    row, col, core = (lax.axis_index(name) for name in ("row", "col", "sub"))
    seat = col * cores + core
    block = row * cols + col

    def load(frame, tile):
        lanes = pl.ds(tile * chunk, chunk)
        return pltpu.make_async_copy(
            pixels.at[frame, :, lanes], loaded.at[frame, :, lanes], load_sem.at[frame, tile]
        )

    for frame in range(frames):
        for tile in range(cols):
            load(frame, tile).start()
    fetches = [
        pltpu.make_async_copy(far, near, table_sem.at[index])
        for index, (far, near) in enumerate(
            (
                (constants.at[pl.ds(0, tables.shape[0])], tables),
                (
                    constants.at[
                        pl.ds(tables.shape[0], coarse.shape[0]), pl.ds(0, coarse.shape[1])
                    ],
                    coarse,
                ),
            )
        )
    ]
    for copy in fetches:
        copy.start()

    for ref in (above, below, second, side_in, row_in):
        ref[...] = jnp.zeros_like(ref)

    barrier = pltpu.get_barrier_semaphore()
    everyone = rows * team
    here = row * team + seat

    def greet(step):
        other = lax.rem(here + step, everyone)
        pl.semaphore_signal(
            barrier,
            inc=1,
            device_id={
                "row": other // team,
                "col": lax.rem(other, team) // cores,
                "sub": lax.rem(other, cores),
            },
            device_id_type=MESH,
        )

    each(everyone, greet)

    pixel = lax.broadcasted_iota(jnp.int32, (chunk, SUBN), 0)
    lane = lax.broadcasted_iota(jnp.int32, (chunk, SUBN), 1)
    inside = (pixel >> 3) == lane
    offset = (pixel & 7).astype(jnp.float32) - (PIX - 1) / 2.0
    pick_one[...] = jnp.where(inside, 1.0, 0.0).astype(jnp.bfloat16)
    pick_two[:, :SUBN] = jnp.where(inside, offset, 0.0).astype(jnp.bfloat16)
    pick_two[:, SUBN:] = jnp.where(inside, offset * offset, 0.0).astype(jnp.bfloat16)
    line = lax.broadcasted_iota(jnp.int32, (high, pixel_rows), 0)
    pixel = lax.broadcasted_iota(jnp.int32, (high, pixel_rows), 1)
    inside = (pixel >> 3) == line
    offset = (pixel & 7).astype(jnp.float32) - (PIX - 1) / 2.0
    gather = jnp.concatenate(
        [
            jnp.where(inside, 1.0, 0.0),
            jnp.where(inside, offset, 0.0),
            jnp.where(inside, offset * offset, 0.0),
        ],
        0,
    ).astype(jnp.bfloat16)

    def window(across):
        return pl.ds(pl.multiple_of(across * SUBN, SUBN), 2 * SUBN)

    def square(across):
        return pl.ds(pl.multiple_of(across * SUBN, SUBN), SUBN)

    def part_copy(frame, across):
        return pltpu.make_async_remote_copy(
            src_ref=parts.at[frame, :, window(across)],
            dst_ref=stripes.at[seat],
            send_sem=part_sem.at[0, frame, across],
            recv_sem=part_sem.at[1, core, col],
            device_id={"col": across, "sub": frame},
            device_id_type=MESH,
        )

    own_lines = pl.ds(pl.multiple_of(seat * high, 8), high)

    def extra_copy(kind, frame, across):
        return pltpu.make_async_remote_copy(
            src_ref=extras.at[frame, kind, :, square(across)],
            dst_ref=out.at[1 + kind, own_lines, :],
            send_sem=extra_sem.at[kind, 0, frame, across],
            recv_sem=extra_sem.at[kind, 1, core, col],
            device_id={"col": across, "sub": frame},
            device_id_type=MESH,
        )

    def edge_copy(which, frame, across):
        lines = (
            pl.ds(0, MARGIN),
            pl.ds(high - MARGIN, 2 * MARGIN),
            pl.ds(high, MARGIN),
        )[which]
        return pltpu.make_async_remote_copy(
            src_ref=parts.at[frame, lines, window(across)],
            dst_ref=(below, above, second)[which],
            send_sem=edge_sem.at[which, 0, frame, across],
            recv_sem=edge_sem.at[which, 1, 0, 0],
            device_id={"row": row + (-1 if which == 0 else 1), "col": across, "sub": frame},
            device_id_type=MESH,
        )

    edges = [
        (0, (seat == 0) & (row > 0), row < rows - 1),
        (1, (seat == team - 1) & (row < rows - 1), row > 0),
    ]
    if high == MARGIN:
        edges.append((2, (seat == team - 2) & (row < rows - 1), row > 0))

    def members(frame, action):
        for step in range(1, cols):
            action(lax.rem(col + step, cols))
        pl.when(core != frame)(lambda: action(col))

    def senders(action):
        def one(step):
            other = lax.rem(seat + step, team)
            action(lax.rem(other, cores), other // cores)

        each(team, one)

    line = lax.broadcasted_iota(jnp.int32, (high, wide), 0)
    column = lax.broadcasted_iota(jnp.int32, (high, wide), 1)
    stripe = row * team + seat
    for frame in range(frames):
        summed = []
        for tile in range(cols):
            load(frame, tile).wait()
            summed.append(dot(gather, loaded[frame, :, tile * chunk : (tile + 1) * chunk]))
        near, far = split_bf16(
            jnp.concatenate(
                [part[kind * high : (kind + 1) * high] for kind in range(3) for part in summed], 0
            )
        )
        tall = cols * high
        ones = dot(jnp.concatenate([near, far], 0), pick_one[...])
        ones = ones[: 3 * tall] + ones[3 * tall :]
        twos = dot(jnp.concatenate([near[:tall], far[:tall]], 0), pick_two[...])
        twos = twos[:tall] + twos[tall:]
        intensity = ones[:tall]
        scale = 1.0 / intensity
        slope_x = twos[:, :SUBN] * scale
        slope_y = ones[tall : 2 * tall] * scale
        moment_two = twos[:, SUBN:] + ones[2 * tall :]

        def grid(values):
            return jnp.concatenate(
                [values[tile * high : (tile + 1) * high] for tile in range(cols)], 1
            )

        flow_x = jnp.where(column < wide - 1, grid(slope_x), 0.0)
        flow_y = jnp.where(stripe * high + line < rows * SUBN - 1, grid(slope_y), 0.0)
        over = pltpu.roll(flow_y, 1, 0)
        source = pltpu.roll(flow_x, 1, 1) - flow_x - flow_y + jnp.where(line > 0, over, 0.0)
        carried = jnp.where(line == 0, over, 0.0)[:MARGIN]
        both = jnp.concatenate([source, carried], 0)
        both = jnp.concatenate([both, jnp.zeros((high + MARGIN, SUBN), jnp.float32)], 1)
        parts[frame] = pltpu.roll(both, MARGIN, 1)
        if frame == 0:
            pl.semaphore_wait(barrier, everyone - 1)
        members(frame, lambda across: part_copy(frame, across).start())
        for which, sends, _ in edges:

            @pl.when(sends)
            def _():
                for across in range(cols):
                    edge_copy(which, frame, across).start()

        extras[frame, 0] = grid(intensity) * (1.0 / (PIX * PIX))
        extras[frame, 1] = grid(moment_two * scale - slope_x * slope_x - slope_y * slope_y)

    for frame in range(frames):
        for kind in range(2):
            members(frame, lambda across: extra_copy(kind, frame, across).start())

    for copy in fetches:
        copy.wait()
    for lines, source_lines in (
        (slice(0, 2 * SIDE), slice(0, 2 * SIDE)),
        (slice(2 * SIDE, 2 * SIDE + 2 * MARGIN), slice(3 * SIDE, 3 * SIDE + 2 * MARGIN)),
    ):
        halves[0, lines], halves[1, lines] = split_bf16(tables[source_lines])

    stripes[seat] = parts[core, :, window(col)]
    out[1, own_lines, :] = extras[core, 0, :, square(col)]
    out[2, own_lines, :] = extras[core, 1, :, square(col)]

    def part_arrival(of_core, of_col):
        return pltpu.make_async_remote_copy(
            src_ref=stripes.at[0],
            dst_ref=stripes.at[0],
            send_sem=part_sem.at[0, 0, 0],
            recv_sem=part_sem.at[1, of_core, of_col],
            device_id={"col": of_col, "sub": of_core},
            device_id_type=MESH,
        )

    def extra_arrival(kind, of_core, of_col):
        lines = pl.ds(0, high)
        return pltpu.make_async_remote_copy(
            src_ref=out.at[1 + kind, lines, :],
            dst_ref=out.at[1 + kind, lines, :],
            send_sem=extra_sem.at[kind, 0, 0, 0],
            recv_sem=extra_sem.at[kind, 1, of_core, of_col],
            device_id={"col": of_col, "sub": of_core},
            device_id_type=MESH,
        )

    senders(lambda of_core, of_col: part_arrival(of_core, of_col).wait_recv())
    for which, _, receives in edges:

        @pl.when(receives)
        def _():
            edge_copy(which, 0, 0).wait_recv()

    top = above[:MARGIN]
    if high == MARGIN:
        top = top + second[...]
    tiles = [top]
    carry = above[MARGIN:]
    for index in range(team):
        tiles.append(stripes[index, :MARGIN] + carry)
        if high > MARGIN:
            tiles.append(stripes[index, MARGIN:high])
        carry = stripes[index, high:]
    tiles.append(below[...] + carry)
    total = jnp.concatenate(tiles, 0)
    middle = jnp.sum(total[MARGIN : MARGIN + SUBN].reshape(SUBN // 8, 8, 2 * SUBN), 0)
    lane = lax.broadcasted_iota(jnp.int32, (8, SUBN), 1)
    sums[block] = jnp.where(lane < MARGIN, middle[:, SUBN:], middle[:, :SUBN])

    def sum_copy(step):
        to = lax.rem(block + step, blocks)
        return pltpu.make_async_remote_copy(
            src_ref=sums.at[block],
            dst_ref=sums.at[block],
            send_sem=sum_sem.at[0, step],
            recv_sem=sum_sem.at[1, step],
            device_id={"row": to // cols, "col": lax.rem(to, cols)},
            device_id_type=MESH,
        )

    each(blocks, lambda step: sum_copy(step).start())

    vectors, last, rims = (
        (halves[0, lines, :lanes], halves[1, lines, :lanes])
        for lines, lanes in (
            (slice(0, SIDE), SIDE),
            (slice(SIDE, 2 * SIDE), 2 * SUBN),
            (slice(2 * SIDE, 2 * SIDE + 2 * MARGIN), SIDE),
        )
    )
    inverse = tables[2 * SIDE : 3 * SIDE, :SIDE]
    data = split_bf16(total[:, :SIDE])
    data = split_bf16(dot_three(data, vectors))
    data = dot_three(vectors, data) * inverse
    data = split_bf16(dot_three(vectors, split_bf16(data)))
    sides = dot_three(
        rims,
        (data[0][MARGIN : MARGIN + SUBN], data[1][MARGIN : MARGIN + SUBN]),
        ((1,), (1,)),
    )
    rim_out[...] = sides
    solved = dot_three(data, last)
    for index, lines in enumerate((slice(0, MARGIN), slice(SUBN + MARGIN, SIDE))):
        ends = solved[lines, SUBN:]
        row_out[index, 0] = jnp.where(lane >= SUBN - MARGIN, ends, 0.0)
        row_out[index, 1] = solved[lines, :SUBN]
        row_out[index, 2] = jnp.where(lane < MARGIN, ends, 0.0)

    moves = []
    for down in (-1, 0, 1):
        for right in (-1, 0, 1):
            if down == 0 and right == 0:
                continue
            number = (down + 1) * 3 + right + 1
            if down == 0:
                src = rim_out.at[pl.ds(MARGIN if right > 0 else 0, MARGIN)]
                dst = side_in.at[pl.ds(0 if right > 0 else SUBN - MARGIN, MARGIN)]
            else:
                src = row_out.at[(down + 1) // 2, right + 1]
                dst = row_in.at[(down + 1) // 2, right + 1]
            copy = pltpu.make_async_remote_copy(
                src_ref=src,
                dst_ref=dst,
                send_sem=fold_sem.at[0, number],
                recv_sem=fold_sem.at[1, number],
                device_id={"row": row + down, "col": col + right},
                device_id_type=MESH,
            )

            def exists(sign):
                test = row >= 0
                if down:
                    at = row + sign * down
                    test = test & (at >= 0) & (at < rows)
                if right:
                    at = col + sign * right
                    test = test & (at >= 0) & (at < cols)
                return test

            moves.append((copy, exists(1), exists(-1)))

    for copy, sends, _ in moves:
        pl.when(sends)(copy.start)

    each(blocks, lambda step: sum_copy(step).wait_recv())
    mix = sums[0] * coarse[block, 0]
    for index in range(1, blocks):
        mix = mix + sums[index] * coarse[block, index]
    lift = jnp.sum(jnp.sum(mix, 0, keepdims=True), 1, keepdims=True)
    mine = solved[MARGIN : MARGIN + SUBN, :SUBN] + lift

    for copy, _, receives in moves:
        pl.when(receives)(copy.wait_recv)
    mine = mine + side_in[...].T
    out[0] = jnp.concatenate(
        [
            mine[:MARGIN] + row_in[1, 0] + row_in[1, 1] + row_in[1, 2],
            mine[MARGIN : SUBN - MARGIN],
            mine[SUBN - MARGIN :] + row_in[0, 0] + row_in[0, 1] + row_in[0, 2],
        ],
        0,
    )

    for kind in range(2):
        senders(lambda of_core, of_col: extra_arrival(kind, of_core, of_col).wait_recv())
    for frame in range(frames):
        members(frame, lambda across: part_copy(frame, across).wait_send())
        for kind in range(2):
            members(frame, lambda across: extra_copy(kind, frame, across).wait_send())
        for which, sends, _ in edges:

            @pl.when(sends)
            def _():
                for across in range(cols):
                    edge_copy(which, frame, across).wait_send()

    each(blocks, lambda step: sum_copy(step).wait_send())
    for copy, sends, _ in moves:
        pl.when(sends)(copy.wait_send)


def body(sizes, pixels):
    rows, cols, cores = sizes
    frames, pixel_rows, pixel_cols = pixels.shape
    high = pixel_rows // PIX
    wide = pixel_cols // PIX
    team = cols * cores
    blocks = rows * cols
    vmem = pl.BlockSpec(memory_space=pltpu.VMEM)
    hbm = pl.BlockSpec(memory_space=pltpu.HBM)
    tables = host_tables()
    coarse = coarse_inverse(rows, cols)
    constants = np.zeros((2304, 2 * SUBN), np.float32)
    constants[: tables.shape[0]] = tables
    constants[tables.shape[0] : tables.shape[0] + blocks, : coarse.shape[1]] = coarse
    dma = pltpu.SemaphoreType.DMA
    results = pl.pallas_call(
        functools.partial(kernel, sizes),
        out_shape=jax.ShapeDtypeStruct((3, SUBN, SUBN), jnp.float32),
        in_specs=[hbm] * 2,
        out_specs=vmem,
        scratch_shapes=[
            pltpu.VMEM((frames, pixel_rows, pixel_cols), jnp.bfloat16),
            pltpu.VMEM(tables.shape, jnp.float32),
            pltpu.VMEM((2, 2 * SIDE + 2 * MARGIN, 2 * SUBN), jnp.bfloat16),
            pltpu.SMEM(coarse.shape, jnp.float32),
            pltpu.VMEM((SUBN * PIX, SUBN), jnp.bfloat16),
            pltpu.VMEM((SUBN * PIX, 2 * SUBN), jnp.bfloat16),
            pltpu.VMEM((frames, high + MARGIN, wide + SUBN), jnp.float32),
            pltpu.VMEM((frames, 2, high, wide), jnp.float32),
            pltpu.VMEM((team, high + MARGIN, 2 * SUBN), jnp.float32),
            pltpu.VMEM((2 * MARGIN, 2 * SUBN), jnp.float32),
            pltpu.VMEM((MARGIN, 2 * SUBN), jnp.float32),
            pltpu.VMEM((MARGIN, 2 * SUBN), jnp.float32),
            pltpu.VMEM((blocks, 8, SUBN), jnp.float32),
            pltpu.VMEM((2 * MARGIN, SUBN), jnp.float32),
            pltpu.VMEM((2, 3, MARGIN, SUBN), jnp.float32),
            pltpu.VMEM((SUBN, SUBN), jnp.float32),
            pltpu.VMEM((2, 3, MARGIN, SUBN), jnp.float32),
            dma((frames, cols)),
            dma((2,)),
            dma((2, cores, cols)),
            dma((2, 2, cores, cols)),
            dma((3, 2, cores, cols)),
            dma((2, blocks)),
            dma((2, 9)),
        ],
        compiler_params=pltpu.CompilerParams(
            collective_id=0, has_side_effects=True, vmem_limit_bytes=53 * 1024 * 1024
        ),
        name="schwarz",
    )(pixels, constants)
    return tuple(results[index : index + 1] for index in range(3))


def solution(mesh):
    sizes = tuple(mesh.shape[name] for name in ("row", "col", "sub"))
    out = P(("groups", "sub"), "row", "col")
    return jax.shard_map(
        functools.partial(body, sizes),
        mesh=mesh,
        in_specs=(P("groups", ("row", "col", "sub"), None),),
        out_specs=(out, out, out),
        check_vma=False,
    )
```

```python
import functools
import math

import jax
import jax.numpy as jnp
import numpy as np
from jax import lax
from jax.experimental import pallas as pl
from jax.experimental.pallas import tpu as pltpu
from jax.sharding import PartitionSpec as P

PIX = 8
SUBN = 128
MARGIN = 8
SIDE = SUBN + 2 * MARGIN
damping = 2e-05
MESH = pl.DeviceIdType.MESH


def split_bf16(values):
    high = values.astype(jnp.bfloat16)
    return high, (values - high.astype(jnp.float32)).astype(jnp.bfloat16)


def dot(left, right, contract=((1,), (0,))):
    return lax.dot_general(left, right, (contract, ((), ())), preferred_element_type=jnp.float32)


def dot_three(left, right, contract=((1,), (0,))):
    (left_high, left_low), (right_high, right_low) = left, right
    return (
        dot(left_high, right_high, contract)
        + dot(left_low, right_high, contract)
        + dot(left_high, right_low, contract)
    )


def host_tables():
    order = np.arange(1, SIDE + 1, dtype=np.float64)
    vectors = np.sqrt(2.0 / (SIDE + 1)) * np.sin(math.pi * np.outer(order, order) / (SIDE + 1))
    spectrum = 2.0 - 2.0 * np.cos(math.pi * order / (SIDE + 1))
    inverse = 1.0 / (spectrum[:, None] + spectrum[None, :] + damping)
    corner = np.zeros((SIDE, SUBN))
    corner[:, :MARGIN] = vectors[:, SUBN + MARGIN :]
    corner[:, SUBN - MARGIN :] = vectors[:, :MARGIN]
    last = np.concatenate([vectors[:, MARGIN : MARGIN + SUBN], corner], 1)
    rims = np.concatenate([vectors[:MARGIN], vectors[SUBN + MARGIN :]], 0)
    wide = [np.pad(part, ((0, 0), (0, 2 * SUBN - part.shape[1]))) for part in (vectors, inverse, rims)]
    return np.concatenate([wide[0], last, wide[1], wide[2]], 0).astype(np.float32)


def coarse_inverse(blocks_down, blocks_across):
    number = blocks_down * blocks_across
    labels = np.arange(number)
    down, across = labels // blocks_across, labels % blocks_across
    apart = np.abs(down[:, None] - down[None, :]) + np.abs(across[:, None] - across[None, :])
    touching = (apart == 1).astype(np.float64)
    laplace = np.diag(touching.sum(1)) - touching
    matrix = SUBN * laplace + damping * SUBN * SUBN * np.eye(number)
    root = np.linalg.inv(np.linalg.cholesky(matrix))
    spare = max(SUBN - number, 0)
    return np.pad(root.T @ root, ((0, 0), (0, spare))).astype(np.float32)


def each(count, step):
    if count <= 16:
        for index in range(1, count):
            step(index)
    else:
        pl.loop(1, count)(step)


def kernel(
    sizes,
    pixels,
    constants,
    out,
    loaded,
    tables,
    halves,
    coarse,
    pick_one,
    pick_two,
    parts,
    extras,
    stripes,
    above,
    below,
    second,
    sums,
    rim_out,
    row_out,
    side_in,
    row_in,
    load_sem,
    table_sem,
    part_sem,
    extra_sem,
    edge_sem,
    sum_sem,
    fold_sem,
):
    rows, cols, cores = sizes
    frames, pixel_rows, pixel_cols = pixels.shape
    high = pixel_rows // PIX
    wide = pixel_cols // PIX
    team = cols * cores
    blocks = rows * cols
    chunk = SUBN * PIX
    row, col, core = (lax.axis_index(name) for name in ("row", "col", "sub"))
    seat = col * cores + core
    block = row * cols + col

    def load(frame, tile):
        lanes = pl.ds(tile * chunk, chunk)
        return pltpu.make_async_copy(
            pixels.at[frame, :, lanes], loaded.at[frame, :, lanes], load_sem.at[frame, tile]
        )

    for frame in range(frames):
        for tile in range(cols):
            load(frame, tile).start()
    fetches = [
        pltpu.make_async_copy(far, near, table_sem.at[index])
        for index, (far, near) in enumerate(
            (
                (constants.at[pl.ds(0, tables.shape[0])], tables),
                (
                    constants.at[
                        pl.ds(tables.shape[0], coarse.shape[0]), pl.ds(0, coarse.shape[1])
                    ],
                    coarse,
                ),
            )
        )
    ]
    for copy in fetches:
        copy.start()

    for ref in (above, below, second, side_in, row_in):
        ref[...] = jnp.zeros_like(ref)

    barrier = pltpu.get_barrier_semaphore()
    everyone = rows * team
    here = row * team + seat

    def greet(step):
        other = lax.rem(here + step, everyone)
        pl.semaphore_signal(
            barrier,
            inc=1,
            device_id={
                "row": other // team,
                "col": lax.rem(other, team) // cores,
                "sub": lax.rem(other, cores),
            },
            device_id_type=MESH,
        )

    each(everyone, greet)

    pixel = lax.broadcasted_iota(jnp.int32, (chunk, SUBN), 0)
    lane = lax.broadcasted_iota(jnp.int32, (chunk, SUBN), 1)
    inside = (pixel >> 3) == lane
    offset = (pixel & 7).astype(jnp.float32) - (PIX - 1) / 2.0
    pick_one[...] = jnp.where(inside, 1.0, 0.0).astype(jnp.bfloat16)
    pick_two[:, :SUBN] = jnp.where(inside, offset, 0.0).astype(jnp.bfloat16)
    pick_two[:, SUBN:] = jnp.where(inside, offset * offset, 0.0).astype(jnp.bfloat16)
    line = lax.broadcasted_iota(jnp.int32, (high, pixel_rows), 0)
    pixel = lax.broadcasted_iota(jnp.int32, (high, pixel_rows), 1)
    inside = (pixel >> 3) == line
    offset = (pixel & 7).astype(jnp.float32) - (PIX - 1) / 2.0
    gather = jnp.concatenate(
        [
            jnp.where(inside, 1.0, 0.0),
            jnp.where(inside, offset, 0.0),
            jnp.where(inside, offset * offset, 0.0),
        ],
        0,
    ).astype(jnp.bfloat16)

    def square(across):
        return pl.ds(pl.multiple_of(across * SUBN, SUBN), SUBN)

    def part_copy(frame, across):
        return pltpu.make_async_remote_copy(
            src_ref=parts.at[frame, across, pl.ds(0, high + 2 * MARGIN)],
            dst_ref=stripes.at[seat],
            send_sem=part_sem.at[0, frame, across],
            recv_sem=part_sem.at[1, core, col],
            device_id={"col": across, "sub": frame},
            device_id_type=MESH,
        )

    own_lines = pl.ds(pl.multiple_of(seat * high, 8), high)

    def extra_copy(kind, frame, across):
        return pltpu.make_async_remote_copy(
            src_ref=extras.at[frame, kind, :, square(across)],
            dst_ref=out.at[1 + kind, own_lines, :],
            send_sem=extra_sem.at[kind, 0, frame, across],
            recv_sem=extra_sem.at[kind, 1, core, col],
            device_id={"col": across, "sub": frame},
            device_id_type=MESH,
        )

    def edge_copy(which, frame, across):
        lines = (
            pl.ds(0, 2 * MARGIN),
            pl.ds(high, 3 * MARGIN),
            pl.ds(high + MARGIN, 2 * MARGIN),
        )[which]
        return pltpu.make_async_remote_copy(
            src_ref=parts.at[frame, across, lines],
            dst_ref=(below, above, second)[which],
            send_sem=edge_sem.at[which, 0, frame, across],
            recv_sem=edge_sem.at[which, 1, 0, 0],
            device_id={"row": row + (-1 if which == 0 else 1), "col": across, "sub": frame},
            device_id_type=MESH,
        )

    edges = [
        (0, (seat == 0) & (row > 0), row < rows - 1),
        (1, (seat == team - 1) & (row < rows - 1), row > 0),
    ]
    if high == MARGIN:
        edges.append((2, (seat == team - 2) & (row < rows - 1), row > 0))

    def members(frame, action):
        for step in range(1, cols):
            action(lax.rem(col + step, cols))
        pl.when(core != frame)(lambda: action(col))

    def senders(action):
        def one(step):
            other = lax.rem(seat + step, team)
            action(lax.rem(other, cores), other // cores)

        each(team, one)

    line = lax.broadcasted_iota(jnp.int32, (high, wide), 0)
    column = lax.broadcasted_iota(jnp.int32, (high, wide), 1)
    stripe = row * team + seat
    lane8 = lax.broadcasted_iota(jnp.int32, (MARGIN, SUBN), 1)
    for frame in range(frames):
        summed = []
        for tile in range(cols):
            load(frame, tile).wait()
            summed.append(dot(gather, loaded[frame, :, tile * chunk : (tile + 1) * chunk]))
        near, far = split_bf16(
            jnp.concatenate(
                [part[kind * high : (kind + 1) * high] for kind in range(3) for part in summed], 0
            )
        )
        tall = cols * high
        ones = dot(near, pick_one[...]) + dot(far, pick_one[...])
        twos = dot(near[:tall], pick_two[...]) + dot(far[:tall], pick_two[...])
        intensity = ones[:tall]
        scale = 1.0 / intensity
        slope_x = twos[:, :SUBN] * scale
        slope_y = ones[tall : 2 * tall] * scale
        moment_two = twos[:, SUBN:] + ones[2 * tall :]

        def grid(values):
            return jnp.concatenate(
                [values[tile * high : (tile + 1) * high] for tile in range(cols)], 1
            )

        flow_x = jnp.where(column < wide - 1, grid(slope_x), 0.0)
        flow_y = jnp.where(stripe * high + line < rows * SUBN - 1, grid(slope_y), 0.0)
        over = pltpu.roll(flow_y, 1, 0)
        source = pltpu.roll(flow_x, 1, 1) - flow_x - flow_y + jnp.where(line > 0, over, 0.0)
        carried = jnp.where(line == 0, over, 0.0)[:MARGIN]
        both = jnp.concatenate([source, carried], 0)
        both = jnp.concatenate([both, jnp.zeros((high + MARGIN, SUBN), jnp.float32)], 1)
        both = pltpu.roll(both, MARGIN, 1)
        for across in range(cols):
            packed = jnp.zeros((MARGIN, SUBN), jnp.float32)
            for group in range(high // MARGIN + 1):
                rest = both[
                    group * MARGIN : (group + 1) * MARGIN,
                    (across + 1) * SUBN : (across + 2) * SUBN,
                ]
                rest = jnp.where(lane8 < 2 * MARGIN, rest, 0.0)
                packed = packed + (pltpu.roll(rest, 2 * MARGIN * group, 1) if group else rest)
            parts[frame, across] = jnp.concatenate(
                [packed, both[:, across * SUBN : (across + 1) * SUBN], packed], 0
            )
        if frame == 0:
            pl.semaphore_wait(barrier, everyone - 1)
        members(frame, lambda across: part_copy(frame, across).start())
        for which, sends, _ in edges:

            @pl.when(sends)
            def _():
                for across in range(cols):
                    edge_copy(which, frame, across).start()

        extras[frame, 0] = grid(intensity) * (1.0 / (PIX * PIX))
        extras[frame, 1] = grid(moment_two * scale - slope_x * slope_x - slope_y * slope_y)

    for frame in range(frames):
        for kind in range(2):
            members(frame, lambda across: extra_copy(kind, frame, across).start())

    for copy in fetches:
        copy.wait()
    for lines, source_lines in (
        (slice(0, 2 * SIDE), slice(0, 2 * SIDE)),
        (slice(2 * SIDE, 2 * SIDE + 2 * MARGIN), slice(3 * SIDE, 3 * SIDE + 2 * MARGIN)),
    ):
        halves[0, lines], halves[1, lines] = split_bf16(tables[source_lines])

    stripes[seat] = parts[core, col, : high + 2 * MARGIN]
    out[1, own_lines, :] = extras[core, 0, :, square(col)]
    out[2, own_lines, :] = extras[core, 1, :, square(col)]

    def part_arrival(of_core, of_col):
        return pltpu.make_async_remote_copy(
            src_ref=stripes.at[0],
            dst_ref=stripes.at[0],
            send_sem=part_sem.at[0, 0, 0],
            recv_sem=part_sem.at[1, of_core, of_col],
            device_id={"col": of_col, "sub": of_core},
            device_id_type=MESH,
        )

    def extra_arrival(kind, of_core, of_col):
        lines = pl.ds(0, high)
        return pltpu.make_async_remote_copy(
            src_ref=out.at[1 + kind, lines, :],
            dst_ref=out.at[1 + kind, lines, :],
            send_sem=extra_sem.at[kind, 0, 0, 0],
            recv_sem=extra_sem.at[kind, 1, of_core, of_col],
            device_id={"col": of_col, "sub": of_core},
            device_id_type=MESH,
        )

    senders(lambda of_core, of_col: part_arrival(of_core, of_col).wait_recv())
    for which, _, receives in edges:

        @pl.when(receives)
        def _():
            edge_copy(which, 0, 0).wait_recv()

    groups = high // MARGIN

    def widen(values, packed, group):
        rest = pltpu.roll(packed, SUBN - 2 * MARGIN * group, 1) if group else packed
        return jnp.concatenate([values, rest], 1)

    top = widen(above[:MARGIN], above[2 * MARGIN :], groups - 1)
    if groups == 1:
        top = top + widen(second[:MARGIN], second[MARGIN:], groups)
    tiles = [top]
    carry = widen(above[MARGIN : 2 * MARGIN], above[2 * MARGIN :], groups)
    for index in range(team):
        packed = stripes[index, :MARGIN]
        for group in range(groups):
            lines = stripes[index, (group + 1) * MARGIN : (group + 2) * MARGIN]
            tile = widen(lines, packed, group)
            tiles.append(tile if group else tile + carry)
        carry = widen(stripes[index, high + MARGIN :], packed, groups)
    tiles.append(widen(below[MARGIN:], below[:MARGIN], 0) + carry)
    total = jnp.concatenate(tiles, 0)
    middle = jnp.sum(total[MARGIN : MARGIN + SUBN].reshape(SUBN // 8, 8, 2 * SUBN), 0)
    lane = lane8
    sums[block] = jnp.where(lane < MARGIN, middle[:, SUBN:], middle[:, :SUBN])

    def sum_copy(step):
        to = lax.rem(block + step, blocks)
        return pltpu.make_async_remote_copy(
            src_ref=sums.at[block],
            dst_ref=sums.at[block],
            send_sem=sum_sem.at[0, step],
            recv_sem=sum_sem.at[1, step],
            device_id={"row": to // cols, "col": lax.rem(to, cols)},
            device_id_type=MESH,
        )

    each(blocks, lambda step: sum_copy(step).start())

    vectors, last, rims = (
        (halves[0, lines, :lanes], halves[1, lines, :lanes])
        for lines, lanes in (
            (slice(0, SIDE), SIDE),
            (slice(SIDE, 2 * SIDE), 2 * SUBN),
            (slice(2 * SIDE, 2 * SIDE + 2 * MARGIN), SIDE),
        )
    )
    inverse = tables[2 * SIDE : 3 * SIDE, :SIDE]
    data = split_bf16(total[:, :SIDE])
    data = split_bf16(dot_three(data, vectors))
    data = dot_three(vectors, data) * inverse
    data = split_bf16(dot_three(vectors, split_bf16(data)))
    sides = dot_three(
        rims,
        (data[0][MARGIN : MARGIN + SUBN], data[1][MARGIN : MARGIN + SUBN]),
        ((1,), (1,)),
    )
    rim_out[...] = sides
    solved = dot_three(data, last)
    for index, lines in enumerate((slice(0, MARGIN), slice(SUBN + MARGIN, SIDE))):
        ends = solved[lines, SUBN:]
        row_out[index, 0] = jnp.where(lane >= SUBN - MARGIN, ends, 0.0)
        row_out[index, 1] = solved[lines, :SUBN]
        row_out[index, 2] = jnp.where(lane < MARGIN, ends, 0.0)

    moves = []
    for down in (-1, 0, 1):
        for right in (-1, 0, 1):
            if down == 0 and right == 0:
                continue
            number = (down + 1) * 3 + right + 1
            if down == 0:
                src = rim_out.at[pl.ds(MARGIN if right > 0 else 0, MARGIN)]
                dst = side_in.at[pl.ds(0 if right > 0 else SUBN - MARGIN, MARGIN)]
            else:
                src = row_out.at[(down + 1) // 2, right + 1]
                dst = row_in.at[(down + 1) // 2, right + 1]
            copy = pltpu.make_async_remote_copy(
                src_ref=src,
                dst_ref=dst,
                send_sem=fold_sem.at[0, number],
                recv_sem=fold_sem.at[1, number],
                device_id={"row": row + down, "col": col + right},
                device_id_type=MESH,
            )

            def exists(sign):
                test = row >= 0
                if down:
                    at = row + sign * down
                    test = test & (at >= 0) & (at < rows)
                if right:
                    at = col + sign * right
                    test = test & (at >= 0) & (at < cols)
                return test

            moves.append((copy, exists(1), exists(-1)))

    for copy, sends, _ in moves:
        pl.when(sends)(copy.start)

    each(blocks, lambda step: sum_copy(step).wait_recv())
    mix = sums[0] * coarse[block, 0]
    for index in range(1, blocks):
        mix = mix + sums[index] * coarse[block, index]
    lift = jnp.sum(jnp.sum(mix, 0, keepdims=True), 1, keepdims=True)
    mine = solved[MARGIN : MARGIN + SUBN, :SUBN] + lift

    for copy, _, receives in moves:
        pl.when(receives)(copy.wait_recv)
    mine = mine + side_in[...].T
    out[0] = jnp.concatenate(
        [
            mine[:MARGIN] + row_in[1, 0] + row_in[1, 1] + row_in[1, 2],
            mine[MARGIN : SUBN - MARGIN],
            mine[SUBN - MARGIN :] + row_in[0, 0] + row_in[0, 1] + row_in[0, 2],
        ],
        0,
    )

    for kind in range(2):
        senders(lambda of_core, of_col: extra_arrival(kind, of_core, of_col).wait_recv())
    for frame in range(frames):
        members(frame, lambda across: part_copy(frame, across).wait_send())
        for kind in range(2):
            members(frame, lambda across: extra_copy(kind, frame, across).wait_send())
        for which, sends, _ in edges:

            @pl.when(sends)
            def _():
                for across in range(cols):
                    edge_copy(which, frame, across).wait_send()

    each(blocks, lambda step: sum_copy(step).wait_send())
    for copy, sends, _ in moves:
        pl.when(sends)(copy.wait_send)


def body(sizes, pixels):
    rows, cols, cores = sizes
    frames, pixel_rows, pixel_cols = pixels.shape
    high = pixel_rows // PIX
    wide = pixel_cols // PIX
    team = cols * cores
    blocks = rows * cols
    vmem = pl.BlockSpec(memory_space=pltpu.VMEM)
    hbm = pl.BlockSpec(memory_space=pltpu.HBM)
    tables = host_tables()
    coarse = coarse_inverse(rows, cols)
    constants = np.zeros((2304, 2 * SUBN), np.float32)
    constants[: tables.shape[0]] = tables
    constants[tables.shape[0] : tables.shape[0] + blocks, : coarse.shape[1]] = coarse
    dma = pltpu.SemaphoreType.DMA
    results = pl.pallas_call(
        functools.partial(kernel, sizes),
        out_shape=jax.ShapeDtypeStruct((3, SUBN, SUBN), jnp.float32),
        in_specs=[hbm] * 2,
        out_specs=vmem,
        scratch_shapes=[
            pltpu.VMEM((frames, pixel_rows, pixel_cols), jnp.bfloat16),
            pltpu.VMEM(tables.shape, jnp.float32),
            pltpu.VMEM((2, 2 * SIDE + 2 * MARGIN, 2 * SUBN), jnp.bfloat16),
            pltpu.SMEM(coarse.shape, jnp.float32),
            pltpu.VMEM((SUBN * PIX, SUBN), jnp.bfloat16),
            pltpu.VMEM((SUBN * PIX, 2 * SUBN), jnp.bfloat16),
            pltpu.VMEM((frames, cols, high + 3 * MARGIN, SUBN), jnp.float32),
            pltpu.VMEM((frames, 2, high, wide), jnp.float32),
            pltpu.VMEM((team, high + 2 * MARGIN, SUBN), jnp.float32),
            pltpu.VMEM((3 * MARGIN, SUBN), jnp.float32),
            pltpu.VMEM((2 * MARGIN, SUBN), jnp.float32),
            pltpu.VMEM((2 * MARGIN, SUBN), jnp.float32),
            pltpu.VMEM((blocks, 8, SUBN), jnp.float32),
            pltpu.VMEM((2 * MARGIN, SUBN), jnp.float32),
            pltpu.VMEM((2, 3, MARGIN, SUBN), jnp.float32),
            pltpu.VMEM((SUBN, SUBN), jnp.float32),
            pltpu.VMEM((2, 3, MARGIN, SUBN), jnp.float32),
            dma((frames, cols)),
            dma((2,)),
            dma((2, cores, cols)),
            dma((2, 2, cores, cols)),
            dma((3, 2, cores, cols)),
            dma((2, blocks)),
            dma((2, 9)),
        ],
        compiler_params=pltpu.CompilerParams(
            collective_id=0, has_side_effects=True, vmem_limit_bytes=53 * 1024 * 1024
        ),
        name="schwarz",
    )(pixels, constants)
    return tuple(results[index : index + 1] for index in range(3))


def solution(mesh):
    sizes = tuple(mesh.shape[name] for name in ("row", "col", "sub"))
    out = P(("groups", "sub"), "row", "col")
    return jax.shard_map(
        functools.partial(body, sizes),
        mesh=mesh,
        in_specs=(P("groups", ("row", "col", "sub"), None),),
        out_specs=(out, out, out),
        check_vma=False,
    )
```
